512 devices in a mesh: section: 4 (over x), dp: 128 (over z, y, core).
Axes of the slice: x: 4, y: 8, z: 8, core: 2. Of those that a mesh axis runs over, the one named last changes fastest.
Arguments:
- saved_input: bfloat16 [4, 16384, 4096], P('section', 'dp'), may hold values from -48 to 48
- upstream: bfloat16 [4, 16384, 4096], P('section', 'dp'), may hold values from -6 to 6
- cotangent: bfloat16 [4, 16384, 4096], P('section', 'dp'), may hold values from -6 to 6
- norm_gain: bfloat16 [4, 4096], P('section'), may hold values from 0.099609375 to 1.8984375
- token_ids: int32 [16384], P('dp'), may hold values from 0 to 1023, as said below
- piece_home: int32 [1024], replicated, may hold values from 0 to 1023, as said below
- piece_table: float32 [1024, 4096], P('dp', 'section'), may hold values from -0.3 to 0.3
- first_moment: float32 [1024, 4096], P('dp', 'section'), may hold values from -2 to 2
- second_moment: float32 [1024, 4096], P('dp', 'section'), may hold values from 0.01 to 1
Outputs:
- passed_grads: bfloat16 [4, 16384, 4096], P('section', 'dp')
- fresh_rows: float32 [16384, 4096], P('dp', 'section')
- new_table: float32 [1024, 4096], P('dp', 'section')
- new_first: float32 [1024, 4096], P('dp', 'section')
- new_second: float32 [1024, 4096], P('dp', 'section')
The draws below stay inside these ranges and needn't reach their ends.
Inputs may be any that keep to these rules, and one draw needn't show every extreme that they name: `token_ids`: among the tokens of one index of dp, at most 2 distinct pieces share a keeper piece_home // 8; on every index some keeper has exactly 2. `piece_home`: A permutation of the storage rows.
All inputs are finite; a program needn't handle non-finite values.
Results may differ from the reference program's by a relative error of at most 0.008.
Values may be sent and summed in bfloat16 or wider, within the bound.
A program may use at most 64 MiB of HBM per device.

```python
import math
import jax
import jax.numpy as jnp
from jax import lax

D = 4096
TOK_DEV = 128
ROWS_DEV = 8
STEP = 10
SECTIONS = 4
TOKENS = 16384
PIECES = 1024
N_DP = 128


def shared_place(key):
    return jax.random.permutation(key, PIECES).astype(jnp.int32)


def token_storage(key):
    key = jax.random.fold_in(key, 5)
    pairs = min(TOK_DEV * 7 // 16, N_DP)
    rank_key = jax.random.fold_in(key, 77)
    owner_rank = jax.random.permutation(rank_key, N_DP).astype(jnp.int32)
    weights = 64 // (1 + owner_rank) + 1

    def one_device(index):
        device_key = jax.random.fold_in(key, index)
        keys = jax.random.split(device_key, 6)
        scores = jax.random.randint(keys[0], (N_DP,), 1, 4096) * weights * N_DP + jnp.arange(N_DP, dtype=jnp.int32)
        chosen = lax.top_k(scores, pairs)[1].astype(jnp.int32)
        row_one = jnp.minimum(jax.random.randint(keys[1], (pairs,), 0, ROWS_DEV), jax.random.randint(keys[2], (pairs,), 0, ROWS_DEV))
        row_two = (row_one + jax.random.randint(keys[3], (pairs,), 1, ROWS_DEV)) % ROWS_DEV
        storage = jnp.concatenate([chosen * ROWS_DEV + row_one, chosen * ROWS_DEV + row_two])
        repeats = storage[jax.random.randint(keys[4], (TOK_DEV - 2 * pairs,), 0, 2 * pairs)]
        every = jnp.concatenate([storage, repeats])
        return every[jax.random.permutation(keys[5], TOK_DEV)]
    return jax.vmap(one_device)(jnp.arange(N_DP, dtype=jnp.int32)).reshape(-1).astype(jnp.int32)


def quiet_tokens(key):
    storage = token_storage(key)
    order = jax.random.permutation(jax.random.fold_in(key, 91), N_DP).astype(jnp.int32)
    quiet = order < max(N_DP // 4, 1)
    return quiet[storage // ROWS_DEV]


def draw_piece_home(key, part):
    place = shared_place(key)
    return jnp.argsort(place, stable=True).astype(jnp.int32)


def draw_token_ids(key, part):
    place = shared_place(key)
    storage = token_storage(key)
    return place[storage].astype(jnp.int32)


def gradient_field(key, silent):
    values = jnp.clip(jax.random.normal(key, (SECTIONS, TOKENS, D), jnp.float32), -6.0, 6.0)
    section_ids = jnp.arange(SECTIONS, dtype=jnp.int32)[:, None]
    zeroed = (section_ids == 0) & silent[None, :]
    return jnp.where(zeroed[:, :, None], 0.0, values).astype(jnp.bfloat16)


def draw_upstream(key, part):
    silent = quiet_tokens(key)
    key = jax.random.fold_in(key, 13)
    return gradient_field(key, silent)


def draw_cotangent(key, part):
    silent = quiet_tokens(key)
    key = jax.random.fold_in(key, 17)
    return gradient_field(key, silent)


def draw_saved_input(key, part):
    key = jax.random.fold_in(key, 7)
    keys = jax.random.split(key, 3)
    base = jnp.clip(jax.random.normal(keys[0], (SECTIONS, TOKENS, D), jnp.float32), -4.0, 4.0)
    rows = 0.3 * jnp.exp(jax.random.uniform(keys[1], (SECTIONS, TOKENS, 1), jnp.float32, 0.0, math.log(10.0)))
    cols = 0.4 * jnp.exp(jax.random.uniform(keys[2], (1, 1, D), jnp.float32, 0.0, math.log(10.0)))
    return (base * rows * cols).astype(jnp.bfloat16)


def steps_of(stream_key, dims, pieces, low, top_value):
    level = 1.0
    for dim, shards_of in pieces:
        heights = jax.random.uniform(jax.random.fold_in(jax.random.fold_in(stream_key, 6), dim), (shards_of,), jnp.float32, low / len(pieces), top_value / len(pieces))
        level = level * jnp.repeat(jnp.exp(heights), dims[dim] // shards_of).reshape((-1,) + (1,) * (len(dims) - 1 - dim))
    return level


def noise(own_key, extent, deviation, limit, cuts=(), kind=jnp.bfloat16):
    loudness = steps_of(own_key, extent, cuts, -0.22, 0.18) if cuts else 1.0
    drawn = jax.random.normal(own_key, extent, jnp.float32) * deviation * loudness
    return jnp.minimum(jnp.maximum(drawn, -limit), limit).astype(kind)


def setup_inputs(seed: int = 0) -> dict:
    arg_keys = jax.random.split(jax.random.key(seed), 10)
    saved_input = draw_saved_input(jax.random.fold_in(arg_keys[9], 71), 0)
    upstream = draw_upstream(jax.random.fold_in(arg_keys[9], 71), 0)
    cotangent = draw_cotangent(jax.random.fold_in(arg_keys[9], 71), 0)
    norm_gain = jnp.clip(1.0 + 0.18 * jax.random.normal(arg_keys[3], (SECTIONS, D), jnp.float32), 0.099609375, 1.8984375).astype(jnp.bfloat16)
    token_ids = draw_token_ids(jax.random.fold_in(arg_keys[9], 71), 0)
    piece_home = draw_piece_home(jax.random.fold_in(arg_keys[9], 71), 0)
    piece_table = noise(arg_keys[6], (PIECES, D), 0.05, 0.3, ((0, 128), (1, 4)), jnp.float32)
    first_moment = noise(arg_keys[7], (PIECES, D), 0.3, 2.0, ((0, 128), (1, 4)), jnp.float32)
    second_moment = jnp.clip(jnp.exp(math.log(1.0) - 4.6051702 * jax.random.uniform(arg_keys[8], (PIECES, D), jnp.float32) ** steps_of(arg_keys[8], (PIECES, D), ((0, 128), (1, 4)), -0.2, 0.2)), 0.01, 1.0)
    return dict(saved_input=saved_input, upstream=upstream, cotangent=cotangent, norm_gain=norm_gain, token_ids=token_ids, piece_home=piece_home, piece_table=piece_table, first_moment=first_moment, second_moment=second_moment)


norm_eps = 1e-05
adam_eps = 1e-08
beta_one = 0.9
beta_two = 0.99
learn_rate = 0.01

def norm_backward(inputs, gain, cotangent, upstream):
    inputs = inputs.astype(jnp.float32)
    scaled = gain.astype(jnp.float32) * cotangent.astype(jnp.float32)
    inverse = lax.rsqrt(lax.optimization_barrier(jnp.mean(inputs * inputs, axis=-1, keepdims=True)) + norm_eps)
    along = lax.optimization_barrier(jnp.mean(inputs * scaled, axis=-1, keepdims=True))
    result = upstream.astype(jnp.float32) + inverse * scaled - inputs * inverse ** 3 * along
    return result.astype(jnp.bfloat16)

def adam_rows(touched, grads, table, first, second):
    first_new = jnp.where(touched, beta_one * first + (1.0 - beta_one) * grads, first)
    second_new = jnp.where(touched, beta_two * second + (1.0 - beta_two) * grads * grads, second)
    fix_one = 1.0 - beta_one ** STEP
    fix_two = 1.0 - beta_two ** STEP
    update = learn_rate * (first_new / fix_one) / (jnp.sqrt(second_new / fix_two) + adam_eps)
    table_new = jnp.where(touched, table - update, table)
    return (table_new, first_new, second_new)

def reference(saved_input, upstream, cotangent, norm_gain, token_ids, piece_home, piece_table, first_moment, second_moment):

    def one_section(items):
        return norm_backward(items[0], items[1][None, :], items[2], items[3])
    input_grad = lax.map(one_section, (saved_input, norm_gain, cotangent, upstream))
    passed_grads = jnp.concatenate([input_grad[1:], jnp.zeros((1, TOKENS, D), jnp.bfloat16)], axis=0)
    home = piece_home[token_ids].astype(jnp.int32)
    row_grad = jnp.zeros((PIECES, D), jnp.float32).at[home].add(input_grad[0].astype(jnp.float32))
    counts = jnp.zeros((PIECES,), jnp.float32).at[home].add(jnp.ones((TOKENS,), jnp.float32))
    touched = (counts > 0.5)[:, None]
    new_table, new_first, new_second = adam_rows(touched, row_grad, piece_table, first_moment, second_moment)
    fresh_rows = new_table[home]
    return (passed_grads, fresh_rows, new_table, new_first, new_second)
```

```python
import functools
import math

import jax
import jax.numpy as jnp
from jax import lax
from jax.experimental import pallas as pl
from jax.experimental.pallas import tpu as pltpu
from jax.sharding import PartitionSpec as P

MESH = pl.DeviceIdType.MESH
STEP = 10

norm_eps = 1e-05
adam_eps = 1e-08
beta_one = 0.9
beta_two = 0.99
learn_rate = 0.01
fix_one = 1.0 - beta_one**STEP
fix_two = 1.0 - beta_two**STEP

F32 = jnp.float32
BF16 = jnp.bfloat16
ROWS = 8
LANES = 128
CHUNKS = 4


def dot(a, b):
    return jnp.dot(a, b, preferred_element_type=F32)


def one_hot(a, b):
    return jnp.where(a == b, 1.0, 0.0).astype(BF16)


def drain(ref, sem):
    pltpu.make_async_copy(ref, ref, sem).wait()


def adam_rows(touched, grads, table, first, second):
    first_new = jnp.where(touched, beta_one * first + (1.0 - beta_one) * grads, first)
    second_new = jnp.where(touched, beta_two * second + (1.0 - beta_two) * grads * grads, second)
    update = learn_rate * (first_new / fix_one) / (jnp.sqrt(second_new / fix_two) + adam_eps)
    table_new = jnp.where(touched, table - update, table)
    return (table_new, first_new, second_new)


def kernel(
    ring,
    x_hbm,
    up_hbm,
    ct_hbm,
    gain_ref,
    tok_ref,
    home_ref,
    table_ref,
    first_ref,
    second_ref,
    passed_ref,
    fresh_ref,
    new_table_ref,
    new_first_ref,
    new_second_ref,
    x_buf,
    up_buf,
    ct_buf,
    grad,
    zeros,
    grad_half,
    by_slot,
    by_token,
    meta_out,
    meta_in,
    meta_turned,
    slots_out,
    slots_in,
    part_out,
    part_in,
    rows_out,
    rows_in,
    back_out,
    back_in,
    in_sem,
    zero_sem,
    quarter_send,
    quarter_recv,
    passed_send,
    passed_recv,
    meta_send,
    meta_recv,
    slots_send,
    slots_recv,
    part_send,
    part_recv,
    rows_send,
    rows_recv,
    back_send,
    back_recv,
):
    peers = 2 * ring
    all_slots = peers * peers
    tokens, width = grad.shape
    half = grad_half.shape[2]
    quarter = 2 * half
    sections = width // quarter
    pieces = home_ref.shape[1]
    chunk = tokens // CHUNKS
    sec = lax.axis_index("section")
    dp = lax.axis_index("dp")
    z, yc = dp // peers, dp % peers
    y, core = yc // 2, yc % 2
    ring_me = (yc, z * 2 + core)
    ring_peer = (
        lambda p: z * peers + p,
        lambda p: (p // 2) * peers + y * 2 + (p % 2),
    )
    line_me = (z, y)
    line_peer = (
        lambda q: q * peers + yc,
        lambda q: z * peers + q * 2 + core,
    )

    def send(src, dst, send_sem, recv_sem, section, index):
        pltpu.make_async_remote_copy(
            src_ref=src,
            dst_ref=dst,
            send_sem=send_sem,
            recv_sem=recv_sem,
            device_id=(section, index),
            device_id_type=MESH,
        ).start()

    def to_ring(h, out, into, send_sem, recv_sem):
        mine = pl.ds(pl.multiple_of(ring_me[h] * peers, peers), peers)

        @pl.loop(1, peers)
        def _(d):
            p = (ring_me[h] + d) % peers
            theirs = pl.ds(pl.multiple_of(p * peers, peers), peers)
            send(out.at[h, theirs], into.at[h, mine], send_sem.at[h], recv_sem.at[h], sec, ring_peer[h](p))

        into[h, mine, :] = out[h, mine, :]

    def ring_wait(h, buf, sem):
        drain(buf.at[h, pl.ds(0, (peers - 1) * peers)], sem.at[h])

    loads = ((x_hbm, x_buf), (ct_hbm, ct_buf), (up_hbm, up_buf))

    def load(c, k):
        rows = pl.ds(c * chunk, chunk)
        return pltpu.make_async_copy(loads[k][0].at[0, rows], loads[k][1].at[rows], in_sem.at[c, k])

    for c in range(CHUNKS):
        for k in range(3):
            load(c, k).start()

    barrier = pltpu.get_barrier_semaphore()

    def greet(section, index):
        pl.semaphore_signal(barrier, inc=1, device_id=(section, index), device_id_type=MESH)

    @pl.loop(1, sections)
    def _(d):
        greet((sec + d) % sections, dp)

    @pl.loop(1, peers)
    def _(d):
        greet(sec, ring_peer[0]((ring_me[0] + d) % peers))

    @pl.loop(1, ring)
    def _(d):
        q = (z + d) % ring
        greet(sec, ring_peer[1](q * 2))
        greet(sec, ring_peer[1](q * 2 + 1))

    piece_of = lax.broadcasted_iota(jnp.int32, (pieces, tokens), 0)
    named = one_hot(piece_of, tok_ref[...])
    line_of = lax.broadcasted_iota(jnp.int32, (16, pieces), 0)
    home = home_ref[...]
    keeper_and_place = jnp.where(line_of == 0, home // ROWS, home % ROWS)
    found = dot(keeper_and_place.astype(F32).astype(BF16), named)
    keeper_row, place_row = found[0:1], found[1:2]
    sub = lax.broadcasted_iota(jnp.int32, (tokens, tokens), 0)
    lane = lax.broadcasted_iota(jnp.int32, (tokens, tokens), 1)

    def as_column(row):
        return jnp.sum(jnp.where(sub == lane, row, 0.0), axis=1, keepdims=True)

    keeper_col, place_col = as_column(keeper_row), as_column(place_row)
    same = keeper_col == keeper_row
    slot_row = jnp.max(jnp.where(same & (place_col < place_row), 1.0, 0.0), axis=0, keepdims=True)
    slot_col = jnp.max(jnp.where(same & (place_row < place_col), 1.0, 0.0), axis=1, keepdims=True)

    def split(keeper, h):
        keeper = keeper.astype(jnp.int32)
        kz, ky, kc = keeper // peers, (keeper // 2) % ring, keeper % 2
        return (ky, kz, kc) if h == 0 else (kz, ky, kc)

    def slot_index(keeper, slot, h):
        near, far, kc = split(keeper, h)
        return (near * 2 + kc) * peers + far * 2 + slot.astype(jnp.int32)

    slot_sub = lax.broadcasted_iota(jnp.int32, (all_slots, tokens), 0)
    slot_lane = lax.broadcasted_iota(jnp.int32, (tokens, all_slots), 1)
    place_lane = lax.broadcasted_iota(jnp.int32, (tokens, LANES), 1)
    for h in range(2):
        spread = one_hot(slot_sub, slot_index(keeper_row, slot_row, h))
        by_slot[h] = spread
        by_token[h] = one_hot(slot_lane, slot_index(keeper_col, slot_col, h))
        far_place = split(keeper_col, h)[1] * ROWS + place_col.astype(jnp.int32)
        meta_out[h] = jnp.minimum(dot(spread, one_hot(place_lane, far_place)), 1.0).astype(BF16)

    pl.semaphore_wait(barrier, (sections - 1) + (peers - 1) + 2 * (ring - 1))
    for h in range(2):
        to_ring(h, meta_out, meta_in, meta_send, meta_recv)

    @pl.when(sec == sections - 1)
    def _():
        zeros[...] = jnp.zeros_like(zeros)
        for c in range(CHUNKS):
            rows = pl.ds(c * chunk, chunk)
            pltpu.make_async_copy(zeros, passed_ref.at[0, rows], zero_sem.at[c]).start()

    step = min(512, width)
    for c in range(CHUNKS):
        for k in range(3):
            load(c, k).wait()

        @pl.loop(0, chunk // 16)
        def _(b):
            rows = pl.ds(pl.multiple_of(c * chunk + b * 16, 16), 16)
            squares = jnp.zeros((16, step), F32)
            products = jnp.zeros((16, step), F32)
            for at in range(0, width, step):
                cols = pl.ds(at, step)
                x = x_buf[rows, cols].astype(F32)
                q = gain_ref[:, cols].astype(F32) * ct_buf[rows, cols].astype(F32)
                squares += x * x
                products += x * q
            inverse = lax.rsqrt(jnp.sum(squares, axis=1, keepdims=True) / width + norm_eps)
            along = jnp.sum(products, axis=1, keepdims=True) / width
            scale = inverse * inverse * inverse * along
            for at in range(0, width, step):
                cols = pl.ds(at, step)
                x = x_buf[rows, cols].astype(F32)
                q = gain_ref[:, cols].astype(F32) * ct_buf[rows, cols].astype(F32)
                up = up_buf[rows, cols].astype(F32)
                grad[rows, cols] = (up + inverse * q - x * scale).astype(BF16)

        rows = pl.ds(c * chunk, chunk)

        @pl.when(sec == 0)
        def _():
            @pl.loop(1, sections)
            def _(d):
                cols = pl.ds(pl.multiple_of(d * quarter, LANES), half)
                send(grad.at[rows, cols], grad_half.at[0, rows], quarter_send, quarter_recv.at[0], d, dp)

            for h in range(2):
                grad_half[h, rows, :] = grad[rows, pl.ds(h * half, half)]

        @pl.when(sec > 0)
        def _():
            send(grad.at[rows], passed_ref.at[0, rows], passed_send, passed_recv, sec - 1, dp)

    @pl.when(sec == 0)
    def _():
        @pl.loop(1, sections)
        def _(d):
            cols = pl.ds(pl.multiple_of(d * quarter + half, LANES), half)
            send(grad.at[:, cols], grad_half.at[1], quarter_send, quarter_recv.at[1], d, dp)

    places = ring * ROWS
    for h in range(2):
        ring_wait(h, meta_in, meta_recv)
        turned = meta_in[h].astype(F32).T[0:places].astype(BF16)
        meta_turned[h] = turned
        if h == 0:
            part_out[h, :, pl.ds(half, LANES)] = dot(turned, jnp.ones((all_slots, LANES), BF16))

    def slots(h):
        @pl.when(sec > 0)
        def _():
            drain(grad_half.at[h], quarter_recv.at[h])

        slots_out[h] = dot(by_slot[h], grad_half[h]).astype(BF16)
        to_ring(h, slots_out, slots_in, slots_send, slots_recv)

    part_width = (half + LANES, half)

    def parts(h):
        ring_wait(h, slots_in, slots_recv)
        part_out[h, :, pl.ds(0, half)] = dot(meta_turned[h], slots_in[h])
        cols = pl.ds(0, part_width[h])

        @pl.loop(1, ring)
        def _(d):
            q = (line_me[h] + d) % ring
            theirs = pl.ds(pl.multiple_of(q * ROWS, ROWS), ROWS)
            send(
                part_out.at[h, theirs, cols],
                part_in.at[h, line_me[h], :, cols],
                part_send.at[h],
                part_recv.at[h],
                sec,
                line_peer[h](q),
            )

        mine = pl.ds(pl.multiple_of(line_me[h] * ROWS, ROWS), ROWS)
        part_in[h, line_me[h], :, cols] = part_out[h, mine, cols]

    def update(h, hits):
        drain(part_in.at[h, pl.ds(0, ring - 1), :, pl.ds(0, part_width[h])], part_recv.at[h])
        total = part_in[h, 0]
        for q in range(1, ring):
            total += part_in[h, q]
        if h == 0:
            hits = total[:, half : half + 1]
        cols = pl.ds(h * half, half)
        table, first, second = adam_rows(
            hits > 0.5, total[:, 0:half], table_ref[:, cols], first_ref[:, cols], second_ref[:, cols]
        )
        new_table_ref[:, cols] = table
        new_first_ref[:, cols] = first
        new_second_ref[:, cols] = second
        mid = half // 2
        rows_out[h] = jnp.concatenate([table[:, 0:mid], table[:, mid:half]], axis=0).astype(BF16)

        @pl.loop(1, ring)
        def _(d):
            q = (line_me[h] + d) % ring
            send(
                rows_out.at[h],
                rows_in.at[h, line_me[h]],
                rows_send.at[h],
                rows_recv.at[h],
                sec,
                line_peer[h](q),
            )

        rows_in[h, line_me[h]] = rows_out[h]
        return hits

    def give_back(h):
        drain(rows_in.at[h, pl.ds(0, ring - 1)], rows_recv.at[h])
        blocks = []
        for q in range(ring):
            packed = rows_in[h, q].astype(F32)
            blocks.append(jnp.concatenate([packed[0:ROWS], packed[ROWS : 2 * ROWS]], axis=1))
        table = jnp.concatenate(blocks, axis=0).astype(BF16)
        back_out[h] = dot(meta_in[h, :, pl.ds(0, places)], table).astype(BF16)
        to_ring(h, back_out, back_in, back_send, back_recv)

    def fresh(h):
        ring_wait(h, back_in, back_recv)
        fresh_ref[:, pl.ds(h * half, half)] = dot(by_token[h], back_in[h])

    slots(0)
    slots(1)
    parts(0)
    hits = update(0, None)
    parts(1)
    give_back(0)
    update(1, hits)
    give_back(1)
    fresh(0)
    fresh(1)

    @pl.when(sec == 0)
    def _():
        drain(grad.at[:, pl.ds(0, width - quarter)], quarter_send)

    @pl.when(sec > 0)
    def _():
        drain(grad, passed_send)

    @pl.when(sec < sections - 1)
    def _():
        drain(passed_ref.at[0], passed_recv)

    @pl.when(sec == sections - 1)
    def _():
        for c in range(CHUNKS):
            rows = pl.ds(c * chunk, chunk)
            pltpu.make_async_copy(zeros, passed_ref.at[0, rows], zero_sem.at[c]).wait()

    for h in range(2):
        ring_wait(h, meta_out, meta_send)
        ring_wait(h, slots_out, slots_send)
        ring_wait(h, back_out, back_send)
        drain(part_in.at[h, pl.ds(0, ring - 1), :, pl.ds(0, part_width[h])], part_send.at[h])
        drain(rows_in.at[h, pl.ds(0, ring - 1)], rows_send.at[h])


def shards(
    ring,
    saved_input,
    upstream,
    cotangent,
    norm_gain,
    token_ids,
    piece_home,
    piece_table,
    first_moment,
    second_moment,
):
    _, tokens, width = saved_input.shape
    rows, quarter = piece_table.shape
    half = quarter // 2
    peers = 2 * ring
    slots = peers * peers
    anywhere = pl.BlockSpec(memory_space=pl.ANY)
    vmem = pl.BlockSpec(memory_space=pltpu.VMEM)
    dma = pltpu.SemaphoreType.DMA
    small = jax.ShapeDtypeStruct((rows, quarter), F32)
    return pl.pallas_call(
        functools.partial(kernel, ring),
        out_shape=(
            jax.ShapeDtypeStruct((1, tokens, width), BF16),
            jax.ShapeDtypeStruct((tokens, quarter), F32),
            small,
            small,
            small,
        ),
        in_specs=[anywhere] * 3 + [vmem] * 6,
        out_specs=(anywhere, vmem, vmem, vmem, vmem),
        scratch_shapes=[
            pltpu.VMEM((tokens, width), BF16),
            pltpu.VMEM((tokens, width), BF16),
            pltpu.VMEM((tokens, width), BF16),
            pltpu.VMEM((tokens, width), BF16),
            pltpu.VMEM((tokens // CHUNKS, width), BF16),
            pltpu.VMEM((2, tokens, half), BF16),
            pltpu.VMEM((2, slots, tokens), BF16),
            pltpu.VMEM((2, tokens, slots), BF16),
            pltpu.VMEM((2, slots, LANES), BF16),
            pltpu.VMEM((2, slots, LANES), BF16),
            pltpu.VMEM((2, ring * ROWS, slots), BF16),
            pltpu.VMEM((2, slots, half), BF16),
            pltpu.VMEM((2, slots, half), BF16),
            pltpu.VMEM((2, ring * ROWS, half + LANES), F32),
            pltpu.VMEM((2, ring, ROWS, half + LANES), F32),
            pltpu.VMEM((2, 2 * ROWS, half // 2), BF16),
            pltpu.VMEM((2, ring, 2 * ROWS, half // 2), BF16),
            pltpu.VMEM((2, slots, half), BF16),
            pltpu.VMEM((2, slots, half), BF16),
            dma((CHUNKS, 3)),
            dma((CHUNKS,)),
            dma,
            dma((2,)),
            dma,
            dma,
        ]
        + [dma((2,))] * 10,
        compiler_params=pltpu.CompilerParams(
            collective_id=0, has_side_effects=True, vmem_limit_bytes=40 * 2**20
        ),
        cost_estimate=pl.CostEstimate(
            flops=2 * 10**8, bytes_accessed=6 * 2**20, transcendentals=0
        ),
    )(
        saved_input,
        upstream,
        cotangent,
        norm_gain,
        token_ids[None, :],
        piece_home[None, :],
        piece_table,
        first_moment,
        second_moment,
    )


def solution(mesh):
    ring = math.isqrt(mesh.shape["dp"] // 2)
    in_specs = (
        P("section", "dp", None),
        P("section", "dp", None),
        P("section", "dp", None),
        P("section", None),
        P("dp"),
        P(),
        P("dp", "section"),
        P("dp", "section"),
        P("dp", "section"),
    )
    out_specs = (
        P("section", "dp", None),
        P("dp", "section"),
        P("dp", "section"),
        P("dp", "section"),
        P("dp", "section"),
    )
    return jax.shard_map(
        functools.partial(shards, ring),
        mesh=mesh,
        in_specs=in_specs,
        out_specs=out_specs,
        check_vma=False,
    )
```

```python
import functools
import math

import jax
import jax.numpy as jnp
from jax import lax
from jax.experimental import pallas as pl
from jax.experimental.pallas import tpu as pltpu
from jax.sharding import PartitionSpec as P

MESH = pl.DeviceIdType.MESH
STEP = 10

norm_eps = 1e-05
adam_eps = 1e-08
beta_one = 0.9
beta_two = 0.99
learn_rate = 0.01
fix_one = 1.0 - beta_one**STEP
fix_two = 1.0 - beta_two**STEP

F32 = jnp.float32
BF16 = jnp.bfloat16
ROWS = 8
LANES = 128
CHUNKS = 4


def dot(a, b):
    return jnp.dot(a, b, preferred_element_type=F32)


def one_hot(a, b):
    return jnp.where(a == b, 1.0, 0.0).astype(BF16)


def drain(ref, sem):
    pltpu.make_async_copy(ref, ref, sem).wait()


def adam_rows(touched, grads, table, first, second):
    first_new = jnp.where(touched, beta_one * first + (1.0 - beta_one) * grads, first)
    second_new = jnp.where(touched, beta_two * second + (1.0 - beta_two) * grads * grads, second)
    update = learn_rate * (first_new / fix_one) / (jnp.sqrt(second_new / fix_two) + adam_eps)
    table_new = jnp.where(touched, table - update, table)
    return (table_new, first_new, second_new)


def kernel(
    ring,
    x_hbm,
    up_hbm,
    ct_hbm,
    gain_hbm,
    tok_hbm,
    home_hbm,
    table_hbm,
    first_hbm,
    second_hbm,
    passed_ref,
    fresh_ref,
    new_table_ref,
    new_first_ref,
    new_second_ref,
    x_buf,
    up_buf,
    ct_buf,
    gain_ref,
    tok_ref,
    home_ref,
    table_ref,
    first_ref,
    second_ref,
    grad,
    zeros,
    grad_half,
    by_slot,
    by_token,
    meta_out,
    meta_in,
    meta_turned,
    slots_out,
    slots_in,
    part_out,
    part_in,
    rows_out,
    rows_in,
    back_out,
    back_in,
    in_sem,
    small_sem,
    zero_sem,
    quarter_send,
    quarter_recv,
    passed_send,
    passed_recv,
    meta_send,
    meta_recv,
    slots_send,
    slots_recv,
    part_send,
    part_recv,
    rows_send,
    rows_recv,
    back_send,
    back_recv,
):
    peers = 2 * ring
    all_slots = peers * peers
    tokens, width = grad.shape
    half = grad_half.shape[2]
    quarter = 2 * half
    sections = width // quarter
    pieces = home_ref.shape[1]
    chunk = tokens // CHUNKS
    sec = lax.axis_index("section")
    dp = lax.axis_index("dp")
    z, yc = dp // peers, dp % peers
    y, core = yc // 2, yc % 2
    ring_me = (yc, z * 2 + core)
    ring_peer = (
        lambda p: z * peers + p,
        lambda p: (p // 2) * peers + y * 2 + (p % 2),
    )
    line_me = (z, y)
    line_peer = (
        lambda q: q * peers + yc,
        lambda q: z * peers + q * 2 + core,
    )

    def send(src, dst, send_sem, recv_sem, section, index):
        pltpu.make_async_remote_copy(
            src_ref=src,
            dst_ref=dst,
            send_sem=send_sem,
            recv_sem=recv_sem,
            device_id=(section, index),
            device_id_type=MESH,
        ).start()

    def to_ring(h, out, into, send_sem, recv_sem):
        mine = pl.ds(pl.multiple_of(ring_me[h] * peers, peers), peers)

        @pl.loop(1, peers)
        def _(d):
            p = (ring_me[h] + d) % peers
            theirs = pl.ds(pl.multiple_of(p * peers, peers), peers)
            send(out.at[h, theirs], into.at[h, mine], send_sem.at[h], recv_sem.at[h], sec, ring_peer[h](p))

        into[h, mine, :] = out[h, mine, :]

    def ring_wait(h, buf, sem):
        drain(buf.at[h, pl.ds(0, (peers - 1) * peers)], sem.at[h])

    loads = ((x_hbm, x_buf), (ct_hbm, ct_buf), (up_hbm, up_buf))

    def load(c, k):
        rows = pl.ds(c * chunk, chunk)
        return pltpu.make_async_copy(loads[k][0].at[0, rows], loads[k][1].at[rows], in_sem.at[c, k])

    small = [
        pltpu.make_async_copy(src, dst, small_sem.at[k])
        for k, (src, dst) in enumerate(
            (
                (tok_hbm, tok_ref),
                (home_hbm, home_ref),
                (gain_hbm, gain_ref),
                (table_hbm, table_ref),
                (first_hbm, first_ref),
                (second_hbm, second_ref),
            )
        )
    ]
    for copy in small[:2]:
        copy.start()
    for c in range(CHUNKS):
        for k in range(3):
            load(c, k).start()
        if c == 0:
            small[2].start()
    for copy in small[3:]:
        copy.start()

    barrier = pltpu.get_barrier_semaphore()

    def greet(section, index):
        pl.semaphore_signal(barrier, inc=1, device_id=(section, index), device_id_type=MESH)

    @pl.loop(1, sections)
    def _(d):
        greet((sec + d) % sections, dp)

    @pl.loop(1, peers)
    def _(d):
        greet(sec, ring_peer[0]((ring_me[0] + d) % peers))

    @pl.loop(1, ring)
    def _(d):
        q = (z + d) % ring
        greet(sec, ring_peer[1](q * 2))
        greet(sec, ring_peer[1](q * 2 + 1))

    small[0].wait()
    small[1].wait()

    piece_of = lax.broadcasted_iota(jnp.int32, (pieces, tokens), 0)
    named = one_hot(piece_of, tok_ref[...])
    line_of = lax.broadcasted_iota(jnp.int32, (16, pieces), 0)
    home = home_ref[...]
    keeper_and_place = jnp.where(line_of == 0, home // ROWS, home % ROWS)
    found = dot(keeper_and_place.astype(F32).astype(BF16), named)
    keeper_row, place_row = found[0:1], found[1:2]
    sub = lax.broadcasted_iota(jnp.int32, (tokens, tokens), 0)
    lane = lax.broadcasted_iota(jnp.int32, (tokens, tokens), 1)

    def as_column(row):
        return jnp.sum(jnp.where(sub == lane, row, 0.0), axis=1, keepdims=True)

    keeper_col, place_col = as_column(keeper_row), as_column(place_row)
    same = keeper_col == keeper_row
    slot_row = jnp.max(jnp.where(same & (place_col < place_row), 1.0, 0.0), axis=0, keepdims=True)
    slot_col = jnp.max(jnp.where(same & (place_row < place_col), 1.0, 0.0), axis=1, keepdims=True)

    def split(keeper, h):
        keeper = keeper.astype(jnp.int32)
        kz, ky, kc = keeper // peers, (keeper // 2) % ring, keeper % 2
        return (ky, kz, kc) if h == 0 else (kz, ky, kc)

    def slot_index(keeper, slot, h):
        near, far, kc = split(keeper, h)
        return (near * 2 + kc) * peers + far * 2 + slot.astype(jnp.int32)

    slot_sub = lax.broadcasted_iota(jnp.int32, (all_slots, tokens), 0)
    slot_lane = lax.broadcasted_iota(jnp.int32, (tokens, all_slots), 1)
    place_lane = lax.broadcasted_iota(jnp.int32, (tokens, LANES), 1)
    for h in range(2):
        spread = one_hot(slot_sub, slot_index(keeper_row, slot_row, h))
        by_slot[h] = spread
        by_token[h] = one_hot(slot_lane, slot_index(keeper_col, slot_col, h))
        far_place = split(keeper_col, h)[1] * ROWS + place_col.astype(jnp.int32)
        meta_out[h] = jnp.minimum(dot(spread, one_hot(place_lane, far_place)), 1.0).astype(BF16)

    pl.semaphore_wait(barrier, (sections - 1) + (peers - 1) + 2 * (ring - 1))
    for h in range(2):
        to_ring(h, meta_out, meta_in, meta_send, meta_recv)

    @pl.when(sec == sections - 1)
    def _():
        zeros[...] = jnp.zeros_like(zeros)
        for c in range(CHUNKS):
            rows = pl.ds(c * chunk, chunk)
            pltpu.make_async_copy(zeros, passed_ref.at[0, rows], zero_sem.at[c]).start()

    step = min(512, width)
    small[2].wait()
    for c in range(CHUNKS):
        for k in range(3):
            load(c, k).wait()

        @pl.loop(0, chunk // 16)
        def _(b):
            rows = pl.ds(pl.multiple_of(c * chunk + b * 16, 16), 16)
            squares = jnp.zeros((16, step), F32)
            products = jnp.zeros((16, step), F32)
            for at in range(0, width, step):
                cols = pl.ds(at, step)
                x = x_buf[rows, cols].astype(F32)
                q = gain_ref[:, cols].astype(F32) * ct_buf[rows, cols].astype(F32)
                squares += x * x
                products += x * q
            inverse = lax.rsqrt(jnp.sum(squares, axis=1, keepdims=True) / width + norm_eps)
            along = jnp.sum(products, axis=1, keepdims=True) / width
            scale = inverse * inverse * inverse * along
            for at in range(0, width, step):
                cols = pl.ds(at, step)
                x = x_buf[rows, cols].astype(F32)
                q = gain_ref[:, cols].astype(F32) * ct_buf[rows, cols].astype(F32)
                up = up_buf[rows, cols].astype(F32)
                grad[rows, cols] = (up + inverse * q - x * scale).astype(BF16)

        rows = pl.ds(c * chunk, chunk)

        @pl.when(sec == 0)
        def _():
            @pl.loop(1, sections)
            def _(d):
                cols = pl.ds(pl.multiple_of(d * quarter, LANES), half)
                send(grad.at[rows, cols], grad_half.at[0, rows], quarter_send, quarter_recv.at[0], d, dp)

            for h in range(2):
                grad_half[h, rows, :] = grad[rows, pl.ds(h * half, half)]

        @pl.when(sec > 0)
        def _():
            send(grad.at[rows], passed_ref.at[0, rows], passed_send, passed_recv, sec - 1, dp)

    @pl.when(sec == 0)
    def _():
        @pl.loop(1, sections)
        def _(d):
            cols = pl.ds(pl.multiple_of(d * quarter + half, LANES), half)
            send(grad.at[:, cols], grad_half.at[1], quarter_send, quarter_recv.at[1], d, dp)

    places = ring * ROWS
    for h in range(2):
        ring_wait(h, meta_in, meta_recv)
        turned = meta_in[h].astype(F32).T[0:places].astype(BF16)
        meta_turned[h] = turned
        if h == 0:
            part_out[h, :, pl.ds(half, LANES)] = dot(turned, jnp.ones((all_slots, LANES), BF16))

    def slots(h):
        @pl.when(sec > 0)
        def _():
            drain(grad_half.at[h], quarter_recv.at[h])

        slots_out[h] = dot(by_slot[h], grad_half[h]).astype(BF16)
        to_ring(h, slots_out, slots_in, slots_send, slots_recv)

    part_width = (half + LANES, half)

    def parts(h):
        ring_wait(h, slots_in, slots_recv)
        part_out[h, :, pl.ds(0, half)] = dot(meta_turned[h], slots_in[h])
        cols = pl.ds(0, part_width[h])

        @pl.loop(1, ring)
        def _(d):
            q = (line_me[h] + d) % ring
            theirs = pl.ds(pl.multiple_of(q * ROWS, ROWS), ROWS)
            send(
                part_out.at[h, theirs, cols],
                part_in.at[h, line_me[h], :, cols],
                part_send.at[h],
                part_recv.at[h],
                sec,
                line_peer[h](q),
            )

        mine = pl.ds(pl.multiple_of(line_me[h] * ROWS, ROWS), ROWS)
        part_in[h, line_me[h], :, cols] = part_out[h, mine, cols]

    def update(h, hits):
        drain(part_in.at[h, pl.ds(0, ring - 1), :, pl.ds(0, part_width[h])], part_recv.at[h])
        total = part_in[h, 0]
        for q in range(1, ring):
            total += part_in[h, q]
        if h == 0:
            hits = total[:, half : half + 1]
        cols = pl.ds(h * half, half)
        table, first, second = adam_rows(
            hits > 0.5, total[:, 0:half], table_ref[:, cols], first_ref[:, cols], second_ref[:, cols]
        )
        new_table_ref[:, cols] = table
        new_first_ref[:, cols] = first
        new_second_ref[:, cols] = second
        mid = half // 2
        rows_out[h] = jnp.concatenate([table[:, 0:mid], table[:, mid:half]], axis=0).astype(BF16)

        @pl.loop(1, ring)
        def _(d):
            q = (line_me[h] + d) % ring
            send(
                rows_out.at[h],
                rows_in.at[h, line_me[h]],
                rows_send.at[h],
                rows_recv.at[h],
                sec,
                line_peer[h](q),
            )

        rows_in[h, line_me[h]] = rows_out[h]
        return hits

    def give_back(h):
        drain(rows_in.at[h, pl.ds(0, ring - 1)], rows_recv.at[h])
        blocks = []
        for q in range(ring):
            packed = rows_in[h, q].astype(F32)
            blocks.append(jnp.concatenate([packed[0:ROWS], packed[ROWS : 2 * ROWS]], axis=1))
        table = jnp.concatenate(blocks, axis=0).astype(BF16)
        back_out[h] = dot(meta_in[h, :, pl.ds(0, places)], table).astype(BF16)
        to_ring(h, back_out, back_in, back_send, back_recv)

    def fresh(h):
        ring_wait(h, back_in, back_recv)
        fresh_ref[:, pl.ds(h * half, half)] = dot(by_token[h], back_in[h])

    slots(0)
    slots(1)
    for copy in small[3:]:
        copy.wait()
    parts(0)
    hits = update(0, None)
    parts(1)
    give_back(0)
    update(1, hits)
    give_back(1)
    fresh(0)
    fresh(1)

    @pl.when(sec == 0)
    def _():
        drain(grad.at[:, pl.ds(0, width - quarter)], quarter_send)

    @pl.when(sec > 0)
    def _():
        drain(grad, passed_send)

    @pl.when(sec < sections - 1)
    def _():
        drain(passed_ref.at[0], passed_recv)

    @pl.when(sec == sections - 1)
    def _():
        for c in range(CHUNKS):
            rows = pl.ds(c * chunk, chunk)
            pltpu.make_async_copy(zeros, passed_ref.at[0, rows], zero_sem.at[c]).wait()

    for h in range(2):
        ring_wait(h, meta_out, meta_send)
        ring_wait(h, slots_out, slots_send)
        ring_wait(h, back_out, back_send)
        drain(part_in.at[h, pl.ds(0, ring - 1), :, pl.ds(0, part_width[h])], part_send.at[h])
        drain(rows_in.at[h, pl.ds(0, ring - 1)], rows_send.at[h])


def hand_out(*refs):
    ins, outs, sems = refs[:5], refs[5:10], refs[10]
    copies = [pltpu.make_async_copy(a, b, sems.at[k]) for k, (a, b) in enumerate(zip(ins, outs))]
    for copy in copies:
        copy.start()
    for copy in copies:
        copy.wait()


def shards(
    ring,
    saved_input,
    upstream,
    cotangent,
    norm_gain,
    token_ids,
    piece_home,
    piece_table,
    first_moment,
    second_moment,
):
    _, tokens, width = saved_input.shape
    rows, quarter = piece_table.shape
    half = quarter // 2
    peers = 2 * ring
    slots = peers * peers
    hbm = pl.BlockSpec(memory_space=pltpu.HBM)
    anywhere = pl.BlockSpec(memory_space=pl.ANY)
    vmem = pl.BlockSpec(memory_space=pltpu.VMEM)
    dma = pltpu.SemaphoreType.DMA
    small = jax.ShapeDtypeStruct((rows, quarter), F32)
    out_shape = (
        jax.ShapeDtypeStruct((1, tokens, width), BF16),
        jax.ShapeDtypeStruct((tokens, quarter), F32),
        small,
        small,
        small,
    )
    arrays = (
        saved_input,
        upstream,
        cotangent,
        norm_gain,
        token_ids[None, :],
        piece_home[None, :],
        piece_table,
        first_moment,
        second_moment,
    )
    results = pl.pallas_call(
        functools.partial(kernel, ring),
        out_shape=out_shape,
        in_specs=[hbm] * 9,
        out_specs=(anywhere, vmem, vmem, vmem, vmem),
        scratch_shapes=[
            pltpu.VMEM((tokens, width), BF16),
            pltpu.VMEM((tokens, width), BF16),
            pltpu.VMEM((tokens, width), BF16),
            pltpu.VMEM((1, width), BF16),
            pltpu.VMEM((1, tokens), jnp.int32),
            pltpu.VMEM((1, piece_home.shape[0]), jnp.int32),
            pltpu.VMEM((rows, quarter), F32),
            pltpu.VMEM((rows, quarter), F32),
            pltpu.VMEM((rows, quarter), F32),
            pltpu.VMEM((tokens, width), BF16),
            pltpu.VMEM((tokens // CHUNKS, width), BF16),
            pltpu.VMEM((2, tokens, half), BF16),
            pltpu.VMEM((2, slots, tokens), BF16),
            pltpu.VMEM((2, tokens, slots), BF16),
            pltpu.VMEM((2, slots, LANES), BF16),
            pltpu.VMEM((2, slots, LANES), BF16),
            pltpu.VMEM((2, ring * ROWS, slots), BF16),
            pltpu.VMEM((2, slots, half), BF16),
            pltpu.VMEM((2, slots, half), BF16),
            pltpu.VMEM((2, ring * ROWS, half + LANES), F32),
            pltpu.VMEM((2, ring, ROWS, half + LANES), F32),
            pltpu.VMEM((2, 2 * ROWS, half // 2), BF16),
            pltpu.VMEM((2, ring, 2 * ROWS, half // 2), BF16),
            pltpu.VMEM((2, slots, half), BF16),
            pltpu.VMEM((2, slots, half), BF16),
            dma((CHUNKS, 3)),
            dma((6,)),
            dma((CHUNKS,)),
            dma,
            dma((2,)),
            dma,
            dma,
        ]
        + [dma((2,))] * 10,
        compiler_params=pltpu.CompilerParams(
            collective_id=0, has_side_effects=True, vmem_limit_bytes=40 * 2**20
        ),
        cost_estimate=pl.CostEstimate(
            flops=2 * 10**8, bytes_accessed=6 * 2**20, transcendentals=0
        ),
    )(*(pltpu.with_memory_space_constraint(array, pltpu.HBM) for array in arrays))
    return pl.pallas_call(
        hand_out,
        out_shape=out_shape,
        in_specs=[anywhere] * 5,
        out_specs=(hbm,) * 5,
        scratch_shapes=[dma((5,))],
        compiler_params=pltpu.CompilerParams(vmem_limit_bytes=40 * 2**20),
        cost_estimate=pl.CostEstimate(flops=0, bytes_accessed=3 * 2**20, transcendentals=0),
    )(*results)


def solution(mesh):
    ring = math.isqrt(mesh.shape["dp"] // 2)
    in_specs = (
        P("section", "dp", None),
        P("section", "dp", None),
        P("section", "dp", None),
        P("section", None),
        P("dp"),
        P(),
        P("dp", "section"),
        P("dp", "section"),
        P("dp", "section"),
    )
    out_specs = (
        P("section", "dp", None),
        P("dp", "section"),
        P("dp", "section"),
        P("dp", "section"),
        P("dp", "section"),
    )
    return jax.shard_map(
        functools.partial(shards, ring),
        mesh=mesh,
        in_specs=in_specs,
        out_specs=out_specs,
        check_vma=False,
    )
```

```python
import functools
import math

import jax
import jax.numpy as jnp
from jax import lax
from jax.experimental import pallas as pl
from jax.experimental.pallas import tpu as pltpu
from jax.sharding import PartitionSpec as P

MESH = pl.DeviceIdType.MESH
STEP = 10

norm_eps = 1e-05
adam_eps = 1e-08
beta_one = 0.9
beta_two = 0.99
learn_rate = 0.01
fix_one = 1.0 - beta_one**STEP
fix_two = 1.0 - beta_two**STEP

F32 = jnp.float32
BF16 = jnp.bfloat16
ROWS = 8
LANES = 128
CHUNKS = 4
PARTS = 4


def dot(a, b):
    return jnp.dot(a, b, preferred_element_type=F32)


def one_hot(a, b):
    return jnp.where(a == b, 1.0, 0.0).astype(BF16)


def drain(ref, sem):
    pltpu.make_async_copy(ref, ref, sem).wait()


def adam_rows(touched, grads, table, first, second):
    first_new = jnp.where(touched, beta_one * first + (1.0 - beta_one) * grads, first)
    second_new = jnp.where(touched, beta_two * second + (1.0 - beta_two) * grads * grads, second)
    update = learn_rate * (first_new / fix_one) / (jnp.sqrt(second_new / fix_two) + adam_eps)
    table_new = jnp.where(touched, table - update, table)
    return (table_new, first_new, second_new)


def kernel(
    ring,
    x_hbm,
    up_hbm,
    ct_hbm,
    gain_hbm,
    tok_hbm,
    home_hbm,
    table_hbm,
    first_hbm,
    second_hbm,
    passed_ref,
    fresh_ref,
    new_table_ref,
    new_first_ref,
    new_second_ref,
    x_buf,
    up_buf,
    ct_buf,
    gain_ref,
    tok_ref,
    home_ref,
    table_ref,
    first_ref,
    second_ref,
    grad,
    zeros,
    grad_part,
    by_slot,
    by_token,
    meta_out,
    meta_in,
    meta_turned,
    slots_out,
    slots_in,
    part_out,
    part_in,
    rows_out,
    rows_in,
    back_out,
    back_in,
    in_sem,
    small_sem,
    zero_sem,
    quarter_send,
    quarter_recv,
    passed_send,
    passed_recv,
    meta_send,
    meta_recv,
    slots_send,
    slots_recv,
    part_send,
    part_recv,
    rows_send,
    rows_recv,
    back_send,
    back_recv,
):
    peers = 2 * ring
    all_slots = peers * peers
    places = ring * ROWS
    tokens, width = grad.shape
    part = grad_part.shape[2]
    mid = part // 2
    quarter = PARTS * part
    sections = width // quarter
    pieces = home_ref.shape[1]
    chunk = tokens // CHUNKS
    sec = lax.axis_index("section")
    dp = lax.axis_index("dp")
    z, yc = dp // peers, dp % peers
    y, core = yc // 2, yc % 2
    ring_me = (yc, z * 2 + core)
    ring_peer = (
        lambda p: z * peers + p,
        lambda p: (p // 2) * peers + y * 2 + (p % 2),
    )
    line_me = (z, y)
    line_peer = (
        lambda q: q * peers + yc,
        lambda q: z * peers + q * 2 + core,
    )

    def send(src, dst, send_sem, recv_sem, section, index):
        pltpu.make_async_remote_copy(
            src_ref=src,
            dst_ref=dst,
            send_sem=send_sem,
            recv_sem=recv_sem,
            device_id=(section, index),
            device_id_type=MESH,
        ).start()

    def farthest_first(k, n):
        return n // 2 + (1 - 2 * (k % 2)) * ((k + 1) // 2)

    def to_ring(way, j, out, into, send_sem, recv_sem):
        mine = pl.ds(pl.multiple_of(ring_me[way] * peers, peers), peers)

        @pl.loop(0, peers - 1)
        def _(k):
            p = (ring_me[way] + farthest_first(k, peers)) % peers
            theirs = pl.ds(pl.multiple_of(p * peers, peers), peers)
            send(out.at[j, theirs], into.at[j, mine], send_sem.at[j], recv_sem.at[j], sec, ring_peer[way](p))

        into[j, mine, :] = out[j, mine, :]

    def ring_wait(j, buf, sem):
        drain(buf.at[j, pl.ds(0, (peers - 1) * peers)], sem.at[j])

    barrier = pltpu.get_barrier_semaphore()

    def greet(section, index):
        pl.semaphore_signal(barrier, inc=1, device_id=(section, index), device_id_type=MESH)

    @pl.loop(1, sections)
    def _(d):
        greet((sec + d) % sections, dp)

    @pl.loop(1, peers)
    def _(d):
        greet(sec, ring_peer[0]((ring_me[0] + d) % peers))

    @pl.loop(1, ring)
    def _(d):
        q = (z + d) % ring
        greet(sec, ring_peer[1](q * 2))
        greet(sec, ring_peer[1](q * 2 + 1))

    loads = ((x_hbm, x_buf), (ct_hbm, ct_buf), (up_hbm, up_buf))

    def load(c, k):
        rows = pl.ds(c * chunk, chunk)
        return pltpu.make_async_copy(loads[k][0].at[0, rows], loads[k][1].at[rows], in_sem.at[c, k])

    small = [
        pltpu.make_async_copy(src, dst, small_sem.at[k])
        for k, (src, dst) in enumerate(
            (
                (gain_hbm, gain_ref),
                (tok_hbm, tok_ref),
                (home_hbm, home_ref),
                (table_hbm, table_ref),
                (first_hbm, first_ref),
                (second_hbm, second_ref),
            )
        )
    ]
    small[0].start()
    for c in range(CHUNKS):
        for k in range(3):
            load(c, k).start()
    for copy in small[1:]:
        copy.start()

    step = min(512, width)

    def norm(c):
        for k in range(3):
            load(c, k).wait()

        @pl.loop(0, chunk // 16)
        def _(b):
            rows = pl.ds(pl.multiple_of(c * chunk + b * 16, 16), 16)
            squares = jnp.zeros((16, step), F32)
            products = jnp.zeros((16, step), F32)
            for at in range(0, width, step):
                cols = pl.ds(at, step)
                x = x_buf[rows, cols].astype(F32)
                q = gain_ref[:, cols].astype(F32) * ct_buf[rows, cols].astype(F32)
                squares += x * x
                products += x * q
            inverse = lax.rsqrt(jnp.sum(squares, axis=1, keepdims=True) / width + norm_eps)
            along = jnp.sum(products, axis=1, keepdims=True) / width
            scale = inverse * inverse * inverse * along
            for at in range(0, width, step):
                cols = pl.ds(at, step)
                x = x_buf[rows, cols].astype(F32)
                q = gain_ref[:, cols].astype(F32) * ct_buf[rows, cols].astype(F32)
                up = up_buf[rows, cols].astype(F32)
                grad[rows, cols] = (up + inverse * q - x * scale).astype(BF16)

    small[0].wait()
    for c in range(CHUNKS):
        norm(c)
    pl.semaphore_wait(barrier, (sections - 1) + (peers - 1) + 2 * (ring - 1))

    last = sections - 1

    def send_quarter(d, j):
        cols = pl.ds(d * quarter + j * part, part)
        send(grad.at[:, cols], grad_part.at[j], quarter_send, quarter_recv.at[j], d, dp)

    @pl.when(sec == 0)
    def _():
        for j in range(PARTS):
            for d in range(1, sections):
                send_quarter(d, j)
        for j in range(PARTS):
            grad_part[j] = grad[:, pl.ds(j * part, part)]

    @pl.when(sec > 0)
    def _():
        send(grad, passed_ref.at[0], passed_send, passed_recv, sec - 1, dp)

    small[1].wait()
    small[2].wait()
    piece_of = lax.broadcasted_iota(jnp.int32, (pieces, tokens), 0)
    named = one_hot(piece_of, tok_ref[...])
    line_of = lax.broadcasted_iota(jnp.int32, (16, pieces), 0)
    home = home_ref[...]
    keeper_and_place = jnp.where(line_of == 0, home // ROWS, home % ROWS)
    found = dot(keeper_and_place.astype(F32).astype(BF16), named)
    keeper_row, place_row = found[0:1], found[1:2]
    sub = lax.broadcasted_iota(jnp.int32, (tokens, tokens), 0)
    lane = lax.broadcasted_iota(jnp.int32, (tokens, tokens), 1)

    def as_column(row):
        return jnp.sum(jnp.where(sub == lane, row, 0.0), axis=1, keepdims=True)

    keeper_col, place_col = as_column(keeper_row), as_column(place_row)
    same = keeper_col == keeper_row
    slot_row = jnp.max(jnp.where(same & (place_col < place_row), 1.0, 0.0), axis=0, keepdims=True)
    slot_col = jnp.max(jnp.where(same & (place_row < place_col), 1.0, 0.0), axis=1, keepdims=True)

    def split(keeper, way):
        keeper = keeper.astype(jnp.int32)
        kz, ky, kc = keeper // peers, (keeper // 2) % ring, keeper % 2
        return (ky, kz, kc) if way == 0 else (kz, ky, kc)

    def slot_index(keeper, slot, way):
        near, far, kc = split(keeper, way)
        return (near * 2 + kc) * peers + far * 2 + slot.astype(jnp.int32)

    slot_sub = lax.broadcasted_iota(jnp.int32, (all_slots, tokens), 0)
    slot_lane = lax.broadcasted_iota(jnp.int32, (tokens, all_slots), 1)
    place_lane = lax.broadcasted_iota(jnp.int32, (tokens, LANES), 1)
    for way in range(2):
        spread = one_hot(slot_sub, slot_index(keeper_row, slot_row, way))
        by_slot[way] = spread
        far_place = split(keeper_col, way)[1] * ROWS + place_col.astype(jnp.int32)
        meta_out[way] = jnp.minimum(dot(spread, one_hot(place_lane, far_place)), 1.0).astype(BF16)
        to_ring(way, way, meta_out, meta_in, meta_send, meta_recv)

    @pl.when(sec == sections - 1)
    def _():
        zeros[...] = jnp.zeros_like(zeros)
        for c in range(CHUNKS):
            rows = pl.ds(c * chunk, chunk)
            pltpu.make_async_copy(zeros, passed_ref.at[0, rows], zero_sem.at[c]).start()

    def slots(j):
        @pl.when(sec > 0)
        def _():
            drain(grad_part.at[j], quarter_recv.at[j])

        slots_out[j] = dot(by_slot[j % 2], grad_part[j]).astype(BF16)
        to_ring(j % 2, j, slots_out, slots_in, slots_send, slots_recv)

    def learn_places(way):
        ring_wait(way, meta_in, meta_recv)
        turned = meta_in[way].astype(F32).T[0:places].astype(BF16)
        meta_turned[way] = turned
        if way == 0:
            part_out[0, :, pl.ds(part, LANES)] = dot(turned, jnp.ones((all_slots, LANES), BF16))

    def part_cols(j):
        return pl.ds(0, part + LANES if j == 0 else part)

    def parts(j):
        way = j % 2
        ring_wait(j, slots_in, slots_recv)
        part_out[j, :, pl.ds(0, part)] = dot(meta_turned[way], slots_in[j])
        cols = part_cols(j)

        @pl.loop(0, ring - 1)
        def _(k):
            q = (line_me[way] + farthest_first(k, ring)) % ring
            theirs = pl.ds(pl.multiple_of(q * ROWS, ROWS), ROWS)
            send(
                part_out.at[j, theirs, cols],
                part_in.at[j, line_me[way], :, cols],
                part_send.at[j],
                part_recv.at[j],
                sec,
                line_peer[way](q),
            )

        mine = pl.ds(pl.multiple_of(line_me[way] * ROWS, ROWS), ROWS)
        part_in[j, line_me[way], :, cols] = part_out[j, mine, cols]

    def update(j, hits):
        way = j % 2
        drain(part_in.at[j, pl.ds(0, ring - 1), :, part_cols(j)], part_recv.at[j])
        total = part_in[j, 0, :, part_cols(j)]
        for q in range(1, ring):
            total += part_in[j, q, :, part_cols(j)]
        if j == 0:
            hits = total[:, part : part + 1]
        cols = pl.ds(j * part, part)
        table, first, second = adam_rows(
            hits > 0.5, total[:, 0:part], table_ref[:, cols], first_ref[:, cols], second_ref[:, cols]
        )
        rows_out[j] = jnp.concatenate([table[:, 0:mid], table[:, mid:part]], axis=0).astype(BF16)

        @pl.loop(0, ring - 1)
        def _(k):
            q = (line_me[way] + farthest_first(k, ring)) % ring
            send(
                rows_out.at[j],
                rows_in.at[j, line_me[way]],
                rows_send.at[j],
                rows_recv.at[j],
                sec,
                line_peer[way](q),
            )

        rows_in[j, line_me[way]] = rows_out[j]
        new_table_ref[:, cols] = table
        new_first_ref[:, cols] = first
        new_second_ref[:, cols] = second
        return hits

    def give_back(j):
        way = j % 2
        drain(rows_in.at[j, pl.ds(0, ring - 1)], rows_recv.at[j])
        blocks = []
        for q in range(ring):
            packed = rows_in[j, q].astype(F32)
            blocks.append(jnp.concatenate([packed[0:ROWS], packed[ROWS : 2 * ROWS]], axis=1))
        table = jnp.concatenate(blocks, axis=0).astype(BF16)
        back_out[j] = dot(meta_in[way, :, pl.ds(0, places)], table).astype(BF16)
        to_ring(way, j, back_out, back_in, back_send, back_recv)

    def fresh(j):
        ring_wait(j, back_in, back_recv)
        fresh_ref[:, pl.ds(j * part, part)] = dot(by_token[j % 2], back_in[j])

    def learn():
        for way in range(2):
            learn_places(way)
            by_token[way] = one_hot(slot_lane, slot_index(keeper_col, slot_col, way))
        for copy in small[3:]:
            copy.wait()

    for j in range(PARTS):
        slots(j)
    learn()
    for j in range(PARTS):
        parts(j)
    hits = None
    for j in range(PARTS):
        hits = update(j, hits)
    for j in range(PARTS):
        give_back(j)
    for j in range(PARTS):
        fresh(j)

    @pl.when(sec == 0)
    def _():
        drain(grad.at[:, pl.ds(0, width - quarter)], quarter_send)

    @pl.when(sec > 0)
    def _():
        drain(grad, passed_send)

    @pl.when(sec < sections - 1)
    def _():
        drain(passed_ref.at[0], passed_recv)

    @pl.when(sec == sections - 1)
    def _():
        for c in range(CHUNKS):
            rows = pl.ds(c * chunk, chunk)
            pltpu.make_async_copy(zeros, passed_ref.at[0, rows], zero_sem.at[c]).wait()

    for way in range(2):
        ring_wait(way, meta_out, meta_send)
    for j in range(PARTS):
        ring_wait(j, slots_out, slots_send)
        ring_wait(j, back_out, back_send)
        drain(part_in.at[j, pl.ds(0, ring - 1), :, part_cols(j)], part_send.at[j])
        drain(rows_in.at[j, pl.ds(0, ring - 1)], rows_send.at[j])


def hand_out(*refs):
    ins, outs, sems = refs[:5], refs[5:10], refs[10]
    copies = [pltpu.make_async_copy(a, b, sems.at[k]) for k, (a, b) in enumerate(zip(ins, outs))]
    for copy in copies:
        copy.start()
    for copy in copies:
        copy.wait()


def shards(
    ring,
    saved_input,
    upstream,
    cotangent,
    norm_gain,
    token_ids,
    piece_home,
    piece_table,
    first_moment,
    second_moment,
):
    _, tokens, width = saved_input.shape
    rows, quarter = piece_table.shape
    part = quarter // PARTS
    peers = 2 * ring
    slots = peers * peers
    hbm = pl.BlockSpec(memory_space=pltpu.HBM)
    anywhere = pl.BlockSpec(memory_space=pl.ANY)
    vmem = pl.BlockSpec(memory_space=pltpu.VMEM)
    dma = pltpu.SemaphoreType.DMA
    small = jax.ShapeDtypeStruct((rows, quarter), F32)
    out_shape = (
        jax.ShapeDtypeStruct((1, tokens, width), BF16),
        jax.ShapeDtypeStruct((tokens, quarter), F32),
        small,
        small,
        small,
    )
    arrays = (
        saved_input,
        upstream,
        cotangent,
        norm_gain,
        token_ids[None, :],
        piece_home[None, :],
        piece_table,
        first_moment,
        second_moment,
    )
    results = pl.pallas_call(
        functools.partial(kernel, ring),
        out_shape=out_shape,
        in_specs=[hbm] * 9,
        out_specs=(anywhere, vmem, vmem, vmem, vmem),
        scratch_shapes=[
            pltpu.VMEM((tokens, width), BF16),
            pltpu.VMEM((tokens, width), BF16),
            pltpu.VMEM((tokens, width), BF16),
            pltpu.VMEM((1, width), BF16),
            pltpu.VMEM((1, tokens), jnp.int32),
            pltpu.VMEM((1, piece_home.shape[0]), jnp.int32),
            pltpu.VMEM((rows, quarter), F32),
            pltpu.VMEM((rows, quarter), F32),
            pltpu.VMEM((rows, quarter), F32),
            pltpu.VMEM((tokens, width), BF16),
            pltpu.VMEM((tokens // CHUNKS, width), BF16),
            pltpu.VMEM((PARTS, tokens, part), BF16),
            pltpu.VMEM((2, slots, tokens), BF16),
            pltpu.VMEM((2, tokens, slots), BF16),
            pltpu.VMEM((2, slots, LANES), BF16),
            pltpu.VMEM((2, slots, LANES), BF16),
            pltpu.VMEM((2, ring * ROWS, slots), BF16),
            pltpu.VMEM((PARTS, slots, part), BF16),
            pltpu.VMEM((PARTS, slots, part), BF16),
            pltpu.VMEM((PARTS, ring * ROWS, part + LANES), F32),
            pltpu.VMEM((PARTS, ring, ROWS, part + LANES), F32),
            pltpu.VMEM((PARTS, 2 * ROWS, part // 2), BF16),
            pltpu.VMEM((PARTS, ring, 2 * ROWS, part // 2), BF16),
            pltpu.VMEM((PARTS, slots, part), BF16),
            pltpu.VMEM((PARTS, slots, part), BF16),
            dma((CHUNKS, 3)),
            dma((6,)),
            dma((CHUNKS,)),
            dma,
            dma((PARTS,)),
            dma,
            dma,
            dma((2,)),
            dma((2,)),
        ]
        + [dma((PARTS,))] * 8,
        compiler_params=pltpu.CompilerParams(
            collective_id=0, has_side_effects=True, vmem_limit_bytes=40 * 2**20
        ),
        cost_estimate=pl.CostEstimate(
            flops=2 * 10**8, bytes_accessed=6 * 2**20, transcendentals=0
        ),
    )(*(pltpu.with_memory_space_constraint(array, pltpu.HBM) for array in arrays))
    return pl.pallas_call(
        hand_out,
        out_shape=out_shape,
        in_specs=[anywhere] * 5,
        out_specs=(hbm,) * 5,
        scratch_shapes=[dma((5,))],
        compiler_params=pltpu.CompilerParams(vmem_limit_bytes=40 * 2**20),
        cost_estimate=pl.CostEstimate(flops=0, bytes_accessed=3 * 2**20, transcendentals=0),
    )(*results)


def solution(mesh):
    ring = math.isqrt(mesh.shape["dp"] // 2)
    in_specs = (
        P("section", "dp", None),
        P("section", "dp", None),
        P("section", "dp", None),
        P("section", None),
        P("dp"),
        P(),
        P("dp", "section"),
        P("dp", "section"),
        P("dp", "section"),
    )
    out_specs = (
        P("section", "dp", None),
        P("dp", "section"),
        P("dp", "section"),
        P("dp", "section"),
        P("dp", "section"),
    )
    return jax.shard_map(
        functools.partial(shards, ring),
        mesh=mesh,
        in_specs=in_specs,
        out_specs=out_specs,
        check_vma=False,
    )
```

```python
import functools
import math

import jax
import jax.numpy as jnp
from jax import lax
from jax.experimental import pallas as pl
from jax.experimental.pallas import tpu as pltpu
from jax.sharding import PartitionSpec as P

MESH = pl.DeviceIdType.MESH
STEP = 10

norm_eps = 1e-05
adam_eps = 1e-08
beta_one = 0.9
beta_two = 0.99
learn_rate = 0.01
fix_one = 1.0 - beta_one**STEP
fix_two = 1.0 - beta_two**STEP

F32 = jnp.float32
BF16 = jnp.bfloat16
ROWS = 8
LANES = 128
CHUNKS = 4
PARTS = 4
EXTRA = ((2, 2), (2, 3))
BUFFERS = PARTS + len(EXTRA)


def dot(a, b):
    return jnp.dot(a, b, preferred_element_type=F32)


def one_hot(a, b):
    return jnp.where(a == b, 1.0, 0.0).astype(BF16)


def drain(ref, sem):
    pltpu.make_async_copy(ref, ref, sem).wait()


def adam_rows(touched, grads, table, first, second):
    first_new = jnp.where(touched, beta_one * first + (1.0 - beta_one) * grads, first)
    second_new = jnp.where(touched, beta_two * second + (1.0 - beta_two) * grads * grads, second)
    update = learn_rate * (first_new / fix_one) / (jnp.sqrt(second_new / fix_two) + adam_eps)
    table_new = jnp.where(touched, table - update, table)
    return (table_new, first_new, second_new)


def kernel(
    ring,
    x_hbm,
    up_hbm,
    ct_hbm,
    gain_hbm,
    tok_hbm,
    home_hbm,
    table_hbm,
    first_hbm,
    second_hbm,
    passed_ref,
    fresh_ref,
    new_table_ref,
    new_first_ref,
    new_second_ref,
    x_buf,
    up_buf,
    ct_buf,
    gain_ref,
    tok_ref,
    home_ref,
    table_ref,
    first_ref,
    second_ref,
    grad,
    zeros,
    grad_part,
    by_slot,
    by_token,
    meta_out,
    meta_in,
    meta_turned,
    slots_out,
    slots_in,
    part_out,
    part_in,
    row_sums,
    total_out,
    total_in,
    rows_out,
    rows_in,
    back_out,
    back_in,
    in_sem,
    small_sem,
    zero_sem,
    quarter_send,
    quarter_recv,
    passed_send,
    passed_recv,
    meta_send,
    meta_recv,
    slots_send,
    slots_recv,
    part_send,
    part_recv,
    rows_send,
    rows_recv,
    back_send,
    back_recv,
    total_send,
    total_recv,
):
    peers = 2 * ring
    all_slots = peers * peers
    places = ring * ROWS
    tokens, width = grad.shape
    part = grad_part.shape[2]
    mid = part // 2
    quarter = PARTS * part
    sections = width // quarter
    pieces = home_ref.shape[1]
    chunk = tokens // CHUNKS
    sec = lax.axis_index("section")
    dp = lax.axis_index("dp")
    z, yc = dp // peers, dp % peers
    y, core = yc // 2, yc % 2
    ring_me = (yc, z * 2 + core)
    ring_peer = (
        lambda p: z * peers + p,
        lambda p: (p // 2) * peers + y * 2 + (p % 2),
    )
    line_me = (z, y)
    line_peer = (
        lambda q: q * peers + yc,
        lambda q: z * peers + q * 2 + core,
    )

    def send(src, dst, send_sem, recv_sem, section, index):
        pltpu.make_async_remote_copy(
            src_ref=src,
            dst_ref=dst,
            send_sem=send_sem,
            recv_sem=recv_sem,
            device_id=(section, index),
            device_id_type=MESH,
        ).start()

    def farthest_first(k, n):
        return n // 2 + (1 - 2 * (k % 2)) * ((k + 1) // 2)

    def to_ring(way, j, out, into, send_sem, recv_sem):
        mine = pl.ds(pl.multiple_of(ring_me[way] * peers, peers), peers)

        @pl.loop(0, peers - 1)
        def _(k):
            p = (ring_me[way] + farthest_first(k, peers)) % peers
            theirs = pl.ds(pl.multiple_of(p * peers, peers), peers)
            send(out.at[j, theirs], into.at[j, mine], send_sem.at[j], recv_sem.at[j], sec, ring_peer[way](p))

        into[j, mine, :] = out[j, mine, :]

    def ring_wait(j, buf, sem):
        drain(buf.at[j, pl.ds(0, (peers - 1) * peers)], sem.at[j])

    barrier = pltpu.get_barrier_semaphore()

    def greet(section, index):
        pl.semaphore_signal(barrier, inc=1, device_id=(section, index), device_id_type=MESH)

    @pl.loop(1, sections)
    def _(d):
        greet((sec + d) % sections, dp)

    @pl.loop(1, peers)
    def _(d):
        greet(sec, ring_peer[0]((ring_me[0] + d) % peers))

    @pl.loop(1, ring)
    def _(d):
        q = (z + d) % ring
        greet(sec, ring_peer[1](q * 2))
        greet(sec, ring_peer[1](q * 2 + 1))

    loads = ((x_hbm, x_buf), (ct_hbm, ct_buf), (up_hbm, up_buf))

    def load(c, k):
        rows = pl.ds(c * chunk, chunk)
        return pltpu.make_async_copy(loads[k][0].at[0, rows], loads[k][1].at[rows], in_sem.at[c, k])

    small = [
        pltpu.make_async_copy(src, dst, small_sem.at[k])
        for k, (src, dst) in enumerate(
            (
                (gain_hbm, gain_ref),
                (tok_hbm, tok_ref),
                (home_hbm, home_ref),
                (table_hbm, table_ref),
                (first_hbm, first_ref),
                (second_hbm, second_ref),
            )
        )
    ]
    small[0].start()
    for c in range(CHUNKS):
        for k in range(3):
            load(c, k).start()
    for copy in small[1:]:
        copy.start()

    step = min(512, width)

    def norm(c):
        for k in range(3):
            load(c, k).wait()

        @pl.loop(0, chunk // 16)
        def _(b):
            rows = pl.ds(pl.multiple_of(c * chunk + b * 16, 16), 16)
            squares = jnp.zeros((16, step), F32)
            products = jnp.zeros((16, step), F32)
            for at in range(0, width, step):
                cols = pl.ds(at, step)
                x = x_buf[rows, cols].astype(F32)
                q = gain_ref[:, cols].astype(F32) * ct_buf[rows, cols].astype(F32)
                squares += x * x
                products += x * q
            inverse = lax.rsqrt(jnp.sum(squares, axis=1, keepdims=True) / width + norm_eps)
            along = jnp.sum(products, axis=1, keepdims=True) / width
            scale = inverse * inverse * inverse * along
            for at in range(0, width, step):
                cols = pl.ds(at, step)
                x = x_buf[rows, cols].astype(F32)
                q = gain_ref[:, cols].astype(F32) * ct_buf[rows, cols].astype(F32)
                up = up_buf[rows, cols].astype(F32)
                grad[rows, cols] = (up + inverse * q - x * scale).astype(BF16)

    small[0].wait()
    for c in range(CHUNKS):
        norm(c)
    pl.semaphore_wait(barrier, (sections - 1) + (peers - 1) + 2 * (ring - 1))

    last = sections - 1

    def has_no(j):
        owners = [d for d, k in EXTRA if k == j]
        if not owners:
            return None
        return functools.reduce(jnp.logical_or, [sec == d for d in owners])

    def where_summed(b, run):
        left = None if b >= PARTS else has_no(b)
        if b >= PARTS:
            pl.when(sec == 0)(run)
        elif left is None:
            run()
        else:
            pl.when(jnp.logical_not(left))(run)

    def part_of(b):
        return b if b < PARTS else EXTRA[b - PARTS][1]

    def send_quarter(d, j):
        cols = pl.ds(d * quarter + j * part, part)
        send(grad.at[:, cols], grad_part.at[j], quarter_send, quarter_recv.at[j], d, dp)

    @pl.when(sec == 0)
    def _():
        for j in range(PARTS):
            for d in range(1, sections):
                if (d, j) not in EXTRA:
                    send_quarter(d, j)
        for j in range(PARTS):
            grad_part[j] = grad[:, pl.ds(j * part, part)]
        for e, (d, j) in enumerate(EXTRA):
            grad_part[PARTS + e] = grad[:, pl.ds(d * quarter + j * part, part)]

    @pl.when(sec > 0)
    def _():
        send(grad, passed_ref.at[0], passed_send, passed_recv, sec - 1, dp)

    small[1].wait()
    small[2].wait()
    piece_of = lax.broadcasted_iota(jnp.int32, (pieces, tokens), 0)
    named = one_hot(piece_of, tok_ref[...])
    line_of = lax.broadcasted_iota(jnp.int32, (16, pieces), 0)
    home = home_ref[...]
    keeper_and_place = jnp.where(line_of == 0, home // ROWS, home % ROWS)
    found = dot(keeper_and_place.astype(F32).astype(BF16), named)
    keeper_row, place_row = found[0:1], found[1:2]
    sub = lax.broadcasted_iota(jnp.int32, (tokens, tokens), 0)
    lane = lax.broadcasted_iota(jnp.int32, (tokens, tokens), 1)

    def as_column(row):
        return jnp.sum(jnp.where(sub == lane, row, 0.0), axis=1, keepdims=True)

    keeper_col, place_col = as_column(keeper_row), as_column(place_row)
    same = keeper_col == keeper_row
    slot_row = jnp.max(jnp.where(same & (place_col < place_row), 1.0, 0.0), axis=0, keepdims=True)
    slot_col = jnp.max(jnp.where(same & (place_row < place_col), 1.0, 0.0), axis=1, keepdims=True)

    def split(keeper, way):
        keeper = keeper.astype(jnp.int32)
        kz, ky, kc = keeper // peers, (keeper // 2) % ring, keeper % 2
        return (ky, kz, kc) if way == 0 else (kz, ky, kc)

    def slot_index(keeper, slot, way):
        near, far, kc = split(keeper, way)
        return (near * 2 + kc) * peers + far * 2 + slot.astype(jnp.int32)

    slot_sub = lax.broadcasted_iota(jnp.int32, (all_slots, tokens), 0)
    slot_lane = lax.broadcasted_iota(jnp.int32, (tokens, all_slots), 1)
    place_lane = lax.broadcasted_iota(jnp.int32, (tokens, LANES), 1)
    for way in range(2):
        spread = one_hot(slot_sub, slot_index(keeper_row, slot_row, way))
        by_slot[way] = spread
        far_place = split(keeper_col, way)[1] * ROWS + place_col.astype(jnp.int32)
        meta_out[way] = jnp.minimum(dot(spread, one_hot(place_lane, far_place)), 1.0).astype(BF16)
        to_ring(way, way, meta_out, meta_in, meta_send, meta_recv)

    @pl.when(sec == sections - 1)
    def _():
        zeros[...] = jnp.zeros_like(zeros)
        for c in range(CHUNKS):
            rows = pl.ds(c * chunk, chunk)
            pltpu.make_async_copy(zeros, passed_ref.at[0, rows], zero_sem.at[c]).start()

    def slots(b):
        way = part_of(b) % 2

        def run():
            if b < PARTS:

                @pl.when(sec > 0)
                def _():
                    drain(grad_part.at[b], quarter_recv.at[b])

            slots_out[b] = dot(by_slot[way], grad_part[b]).astype(BF16)
            to_ring(way, b, slots_out, slots_in, slots_send, slots_recv)

        where_summed(b, run)

    def learn_places(way):
        ring_wait(way, meta_in, meta_recv)
        turned = meta_in[way].astype(F32).T[0:places].astype(BF16)
        meta_turned[way] = turned
        if way == 0:
            hits = dot(turned, jnp.ones((all_slots, LANES), BF16))
            none = jnp.zeros((ROWS, LANES), F32)
            packed = [x for q in range(ring) for x in (hits[q * ROWS : (q + 1) * ROWS], none)]
            part_out[0, :, pl.ds(mid, LANES)] = jnp.concatenate(packed, axis=0).astype(BF16)

    def part_cols(b):
        return pl.ds(0, mid + LANES if b == 0 else mid)

    def pack(rows):
        return jnp.concatenate([rows[:, 0:mid], rows[:, mid:part]], axis=0)

    def unpack(rows):
        return jnp.concatenate([rows[0:ROWS, 0:mid], rows[ROWS : 2 * ROWS, 0:mid]], axis=1)

    def parts(b):
        way = part_of(b) % 2
        cols = part_cols(b)

        def run():
            ring_wait(b, slots_in, slots_recv)
            sums = dot(meta_turned[way], slots_in[b])
            packed = [pack(sums[q * ROWS : (q + 1) * ROWS]) for q in range(ring)]
            part_out[b, :, pl.ds(0, mid)] = jnp.concatenate(packed, axis=0).astype(BF16)

            @pl.loop(0, ring - 1)
            def _(k):
                q = (line_me[way] + farthest_first(k, ring)) % ring
                theirs = pl.ds(pl.multiple_of(q * 2 * ROWS, 2 * ROWS), 2 * ROWS)
                send(
                    part_out.at[b, theirs, cols],
                    part_in.at[b, line_me[way], :, cols],
                    part_send.at[b],
                    part_recv.at[b],
                    sec,
                    line_peer[way](q),
                )

            mine = pl.ds(pl.multiple_of(line_me[way] * 2 * ROWS, 2 * ROWS), 2 * ROWS)
            part_in[b, line_me[way], :, cols] = part_out[b, mine, cols]

        where_summed(b, run)

    def total(b):
        drain(part_in.at[b, pl.ds(0, ring - 1), :, part_cols(b)], part_recv.at[b])
        rows = part_in[b, 0, :, part_cols(b)].astype(F32)
        for q in range(1, ring):
            rows += part_in[b, q, :, part_cols(b)].astype(F32)
        return rows

    def hand_total(e):
        @pl.when(sec == 0)
        def _():
            total_out[e] = unpack(total(PARTS + e))
            send(total_out.at[e], total_in.at[e], total_send.at[e], total_recv.at[e], EXTRA[e][0], dp)

    def update(j, hits):
        way = j % 2
        if has_no(j) is None:
            rows = total(j)
            sums = unpack(rows)
            if j == 0:
                hits = rows[0:ROWS, mid : mid + 1]
        else:

            def run():
                row_sums[...] = unpack(total(j))

            where_summed(j, run)
            for e, (d, k) in enumerate(EXTRA):
                if k == j:

                    @pl.when(sec == d)
                    def _():
                        drain(total_in.at[e], total_recv.at[e])
                        row_sums[...] = total_in[e]

            sums = row_sums[...]
        cols = pl.ds(j * part, part)
        table, first, second = adam_rows(
            hits > 0.5, sums, table_ref[:, cols], first_ref[:, cols], second_ref[:, cols]
        )
        rows_out[j] = pack(table).astype(BF16)

        @pl.loop(0, ring - 1)
        def _(k):
            q = (line_me[way] + farthest_first(k, ring)) % ring
            send(
                rows_out.at[j],
                rows_in.at[j, line_me[way]],
                rows_send.at[j],
                rows_recv.at[j],
                sec,
                line_peer[way](q),
            )

        rows_in[j, line_me[way]] = rows_out[j]
        new_table_ref[:, cols] = table
        new_first_ref[:, cols] = first
        new_second_ref[:, cols] = second
        return hits

    def give_back(j):
        way = j % 2
        drain(rows_in.at[j, pl.ds(0, ring - 1)], rows_recv.at[j])
        blocks = [unpack(rows_in[j, q].astype(F32)) for q in range(ring)]
        table = jnp.concatenate(blocks, axis=0).astype(BF16)
        back_out[j] = dot(meta_in[way, :, pl.ds(0, places)], table).astype(BF16)
        to_ring(way, j, back_out, back_in, back_send, back_recv)

    def fresh(j):
        ring_wait(j, back_in, back_recv)
        fresh_ref[:, pl.ds(j * part, part)] = dot(by_token[j % 2], back_in[j])

    def learn():
        for way in range(2):
            learn_places(way)
            by_token[way] = one_hot(slot_lane, slot_index(keeper_col, slot_col, way))
        for copy in small[3:]:
            copy.wait()

    buffers = (*range(PARTS, PARTS + len(EXTRA)), *range(PARTS))
    for b in buffers:
        slots(b)
    learn()
    for b in buffers:
        parts(b)
    hits = None
    for e in range(len(EXTRA)):
        hand_total(e)
    for j in range(PARTS):
        hits = update(j, hits)
    for j in range(PARTS):
        give_back(j)
    for j in range(PARTS):
        fresh(j)

    @pl.when(sec == 0)
    def _():
        drain(grad.at[:, pl.ds(0, width - quarter - len(EXTRA) * part)], quarter_send)

    @pl.when(sec > 0)
    def _():
        drain(grad, passed_send)

    @pl.when(sec < sections - 1)
    def _():
        drain(passed_ref.at[0], passed_recv)

    @pl.when(sec == sections - 1)
    def _():
        for c in range(CHUNKS):
            rows = pl.ds(c * chunk, chunk)
            pltpu.make_async_copy(zeros, passed_ref.at[0, rows], zero_sem.at[c]).wait()

    for way in range(2):
        ring_wait(way, meta_out, meta_send)
    for j in range(PARTS):
        ring_wait(j, back_out, back_send)
        drain(rows_in.at[j, pl.ds(0, ring - 1)], rows_send.at[j])
    for b in buffers:

        def sent():
            ring_wait(b, slots_out, slots_send)
            drain(part_in.at[b, pl.ds(0, ring - 1), :, part_cols(b)], part_send.at[b])

        where_summed(b, sent)

    @pl.when(sec == 0)
    def _():
        for e in range(len(EXTRA)):
            drain(total_out.at[e], total_send.at[e])


def hand_out(*refs):
    ins, outs, sems = refs[:5], refs[5:10], refs[10]
    copies = [pltpu.make_async_copy(a, b, sems.at[k]) for k, (a, b) in enumerate(zip(ins, outs))]
    for copy in copies:
        copy.start()
    for copy in copies:
        copy.wait()


def shards(
    ring,
    saved_input,
    upstream,
    cotangent,
    norm_gain,
    token_ids,
    piece_home,
    piece_table,
    first_moment,
    second_moment,
):
    _, tokens, width = saved_input.shape
    rows, quarter = piece_table.shape
    part = quarter // PARTS
    peers = 2 * ring
    slots = peers * peers
    hbm = pl.BlockSpec(memory_space=pltpu.HBM)
    anywhere = pl.BlockSpec(memory_space=pl.ANY)
    vmem = pl.BlockSpec(memory_space=pltpu.VMEM)
    dma = pltpu.SemaphoreType.DMA
    small = jax.ShapeDtypeStruct((rows, quarter), F32)
    out_shape = (
        jax.ShapeDtypeStruct((1, tokens, width), BF16),
        jax.ShapeDtypeStruct((tokens, quarter), F32),
        small,
        small,
        small,
    )
    arrays = (
        saved_input,
        upstream,
        cotangent,
        norm_gain,
        token_ids[None, :],
        piece_home[None, :],
        piece_table,
        first_moment,
        second_moment,
    )
    results = pl.pallas_call(
        functools.partial(kernel, ring),
        out_shape=out_shape,
        in_specs=[hbm] * 9,
        out_specs=(anywhere, vmem, vmem, vmem, vmem),
        scratch_shapes=[
            pltpu.VMEM((tokens, width), BF16),
            pltpu.VMEM((tokens, width), BF16),
            pltpu.VMEM((tokens, width), BF16),
            pltpu.VMEM((1, width), BF16),
            pltpu.VMEM((1, tokens), jnp.int32),
            pltpu.VMEM((1, piece_home.shape[0]), jnp.int32),
            pltpu.VMEM((rows, quarter), F32),
            pltpu.VMEM((rows, quarter), F32),
            pltpu.VMEM((rows, quarter), F32),
            pltpu.VMEM((tokens, width), BF16),
            pltpu.VMEM((tokens // CHUNKS, width), BF16),
            pltpu.VMEM((BUFFERS, tokens, part), BF16),
            pltpu.VMEM((2, slots, tokens), BF16),
            pltpu.VMEM((2, tokens, slots), BF16),
            pltpu.VMEM((2, slots, LANES), BF16),
            pltpu.VMEM((2, slots, LANES), BF16),
            pltpu.VMEM((2, ring * ROWS, slots), BF16),
            pltpu.VMEM((BUFFERS, slots, part), BF16),
            pltpu.VMEM((BUFFERS, slots, part), BF16),
            pltpu.VMEM((BUFFERS, ring * 2 * ROWS, part // 2 + LANES), BF16),
            pltpu.VMEM((BUFFERS, ring, 2 * ROWS, part // 2 + LANES), BF16),
            pltpu.VMEM((ROWS, part), F32),
            pltpu.VMEM((len(EXTRA), ROWS, part), F32),
            pltpu.VMEM((len(EXTRA), ROWS, part), F32),
            pltpu.VMEM((PARTS, 2 * ROWS, part // 2), BF16),
            pltpu.VMEM((PARTS, ring, 2 * ROWS, part // 2), BF16),
            pltpu.VMEM((PARTS, slots, part), BF16),
            pltpu.VMEM((PARTS, slots, part), BF16),
            dma((CHUNKS, 3)),
            dma((6,)),
            dma((CHUNKS,)),
            dma,
            dma((PARTS,)),
            dma,
            dma,
            dma((2,)),
            dma((2,)),
        ]
        + [dma((BUFFERS,))] * 4
        + [dma((PARTS,))] * 4
        + [dma((len(EXTRA),))] * 2,
        compiler_params=pltpu.CompilerParams(
            collective_id=0, has_side_effects=True, vmem_limit_bytes=40 * 2**20
        ),
        cost_estimate=pl.CostEstimate(
            flops=2 * 10**8, bytes_accessed=6 * 2**20, transcendentals=0
        ),
    )(*(pltpu.with_memory_space_constraint(array, pltpu.HBM) for array in arrays))
    return pl.pallas_call(
        hand_out,
        out_shape=out_shape,
        in_specs=[anywhere] * 5,
        out_specs=(hbm,) * 5,
        scratch_shapes=[dma((5,))],
        compiler_params=pltpu.CompilerParams(vmem_limit_bytes=40 * 2**20),
        cost_estimate=pl.CostEstimate(flops=0, bytes_accessed=3 * 2**20, transcendentals=0),
    )(*results)


def solution(mesh):
    ring = math.isqrt(mesh.shape["dp"] // 2)
    in_specs = (
        P("section", "dp", None),
        P("section", "dp", None),
        P("section", "dp", None),
        P("section", None),
        P("dp"),
        P(),
        P("dp", "section"),
        P("dp", "section"),
        P("dp", "section"),
    )
    out_specs = (
        P("section", "dp", None),
        P("dp", "section"),
        P("dp", "section"),
        P("dp", "section"),
        P("dp", "section"),
    )
    return jax.shard_map(
        functools.partial(shards, ring),
        mesh=mesh,
        in_specs=in_specs,
        out_specs=out_specs,
        check_vma=False,
    )
```

```python
import functools
import math

import jax
import jax.numpy as jnp
from jax import lax
from jax.experimental import pallas as pl
from jax.experimental.pallas import tpu as pltpu
from jax.sharding import PartitionSpec as P

MESH = pl.DeviceIdType.MESH
STEP = 10

norm_eps = 1e-05
adam_eps = 1e-08
beta_one = 0.9
beta_two = 0.99
learn_rate = 0.01
fix_one = 1.0 - beta_one**STEP
fix_two = 1.0 - beta_two**STEP

F32 = jnp.float32
BF16 = jnp.bfloat16
ROWS = 8
LANES = 128
CHUNKS = 4
PARTS = 4
EXTRA = ((2, 2), (2, 3))
BUFFERS = PARTS + len(EXTRA)


def dot(a, b):
    return jnp.dot(a, b, preferred_element_type=F32)


def one_hot(a, b):
    return jnp.where(a == b, 1.0, 0.0).astype(BF16)


def drain(ref, sem):
    pltpu.make_async_copy(ref, ref, sem).wait()


def adam_rows(touched, grads, table, first, second):
    first_new = jnp.where(touched, beta_one * first + (1.0 - beta_one) * grads, first)
    second_new = jnp.where(touched, beta_two * second + (1.0 - beta_two) * grads * grads, second)
    update = learn_rate * (first_new / fix_one) / (jnp.sqrt(second_new / fix_two) + adam_eps)
    table_new = jnp.where(touched, table - update, table)
    return (table_new, first_new, second_new)


def kernel(
    ring,
    x_hbm,
    up_hbm,
    ct_hbm,
    gain_hbm,
    tok_hbm,
    home_hbm,
    table_hbm,
    first_hbm,
    second_hbm,
    passed_ref,
    fresh_ref,
    new_table_ref,
    new_first_ref,
    new_second_ref,
    x_buf,
    up_buf,
    ct_buf,
    gain_ref,
    tok_ref,
    home_ref,
    table_ref,
    first_ref,
    second_ref,
    grad,
    zeros,
    grad_part,
    by_slot,
    by_token,
    meta_out,
    meta_in,
    meta_turned,
    slots_out,
    slots_in,
    part_out,
    part_in,
    row_sums,
    total_out,
    total_in,
    rows_out,
    rows_in,
    back_out,
    back_in,
    in_sem,
    small_sem,
    zero_sem,
    quarter_send,
    quarter_recv,
    passed_send,
    passed_recv,
    meta_send,
    meta_recv,
    slots_send,
    slots_recv,
    part_send,
    part_recv,
    rows_send,
    rows_recv,
    back_send,
    back_recv,
    total_send,
    total_recv,
):
    peers = 2 * ring
    all_slots = peers * peers
    places = ring * ROWS
    tokens, width = grad.shape
    part = grad_part.shape[2]
    mid = part // 2
    quarter = PARTS * part
    sections = width // quarter
    pieces = home_ref.shape[1]
    chunk = tokens // CHUNKS
    sec = lax.axis_index("section")
    dp = lax.axis_index("dp")
    z, yc = dp // peers, dp % peers
    y, core = yc // 2, yc % 2
    ring_me = (yc, z * 2 + core)
    ring_peer = (
        lambda p: z * peers + p,
        lambda p: (p // 2) * peers + y * 2 + (p % 2),
    )
    line_me = (z, y)
    line_peer = (
        lambda q: q * peers + yc,
        lambda q: z * peers + q * 2 + core,
    )

    def send(src, dst, send_sem, recv_sem, section, index):
        pltpu.make_async_remote_copy(
            src_ref=src,
            dst_ref=dst,
            send_sem=send_sem,
            recv_sem=recv_sem,
            device_id=(section, index),
            device_id_type=MESH,
        ).start()

    def farthest_first(k, n):
        return n // 2 + (1 - 2 * (k % 2)) * ((k + 1) // 2)

    def to_ring(way, j, out, into, send_sem, recv_sem):
        mine = pl.ds(pl.multiple_of(ring_me[way] * peers, peers), peers)

        @pl.loop(0, peers - 1, unroll=True)
        def _(k):
            p = (ring_me[way] + farthest_first(k, peers)) % peers
            theirs = pl.ds(pl.multiple_of(p * peers, peers), peers)
            send(out.at[j, theirs], into.at[j, mine], send_sem.at[j], recv_sem.at[j], sec, ring_peer[way](p))

        into[j, mine, :] = out[j, mine, :]

    def ring_wait(j, buf, sem):
        drain(buf.at[j, pl.ds(0, (peers - 1) * peers)], sem.at[j])

    barrier = pltpu.get_barrier_semaphore()

    def greet(section, index):
        pl.semaphore_signal(barrier, inc=1, device_id=(section, index), device_id_type=MESH)

    @pl.loop(1, sections)
    def _(d):
        greet((sec + d) % sections, dp)

    @pl.loop(1, peers)
    def _(d):
        greet(sec, ring_peer[0]((ring_me[0] + d) % peers))

    @pl.loop(1, ring)
    def _(d):
        q = (z + d) % ring
        greet(sec, ring_peer[1](q * 2))
        greet(sec, ring_peer[1](q * 2 + 1))

    loads = ((x_hbm, x_buf), (ct_hbm, ct_buf), (up_hbm, up_buf))

    def load(c, k):
        rows = pl.ds(c * chunk, chunk)
        return pltpu.make_async_copy(loads[k][0].at[0, rows], loads[k][1].at[rows], in_sem.at[c, k])

    small = [
        pltpu.make_async_copy(src, dst, small_sem.at[k])
        for k, (src, dst) in enumerate(
            (
                (gain_hbm, gain_ref),
                (tok_hbm, tok_ref),
                (home_hbm, home_ref),
                (table_hbm, table_ref),
                (first_hbm, first_ref),
                (second_hbm, second_ref),
            )
        )
    ]
    small[0].start()
    for c in range(CHUNKS):
        for k in range(3):
            load(c, k).start()
    for copy in small[1:]:
        copy.start()

    step = min(512, width)

    def norm(c):
        for k in range(3):
            load(c, k).wait()

        @pl.loop(0, chunk // 16)
        def _(b):
            rows = pl.ds(pl.multiple_of(c * chunk + b * 16, 16), 16)
            squares = jnp.zeros((16, step), F32)
            products = jnp.zeros((16, step), F32)
            for at in range(0, width, step):
                cols = pl.ds(at, step)
                x = x_buf[rows, cols].astype(F32)
                q = gain_ref[:, cols].astype(F32) * ct_buf[rows, cols].astype(F32)
                squares += x * x
                products += x * q
            inverse = lax.rsqrt(jnp.sum(squares, axis=1, keepdims=True) / width + norm_eps)
            along = jnp.sum(products, axis=1, keepdims=True) / width
            scale = inverse * inverse * inverse * along
            for at in range(0, width, step):
                cols = pl.ds(at, step)
                x = x_buf[rows, cols].astype(F32)
                q = gain_ref[:, cols].astype(F32) * ct_buf[rows, cols].astype(F32)
                up = up_buf[rows, cols].astype(F32)
                grad[rows, cols] = (up + inverse * q - x * scale).astype(BF16)

    small[0].wait()
    for c in range(CHUNKS):
        norm(c)
    pl.semaphore_wait(barrier, (sections - 1) + (peers - 1) + 2 * (ring - 1))

    last = sections - 1

    def has_no(j):
        owners = [d for d, k in EXTRA if k == j]
        if not owners:
            return None
        return functools.reduce(jnp.logical_or, [sec == d for d in owners])

    def where_summed(b, run):
        left = None if b >= PARTS else has_no(b)
        if b >= PARTS:
            pl.when(sec == 0)(run)
        elif left is None:
            run()
        else:
            pl.when(jnp.logical_not(left))(run)

    def part_of(b):
        return b if b < PARTS else EXTRA[b - PARTS][1]

    def send_quarter(d, j):
        cols = pl.ds(d * quarter + j * part, part)
        send(grad.at[:, cols], grad_part.at[j], quarter_send, quarter_recv.at[j], d, dp)

    @pl.when(sec == 0)
    def _():
        for j in range(PARTS):
            for d in range(1, sections):
                if (d, j) not in EXTRA:
                    send_quarter(d, j)
        for j in range(PARTS):
            grad_part[j] = grad[:, pl.ds(j * part, part)]
        for e, (d, j) in enumerate(EXTRA):
            grad_part[PARTS + e] = grad[:, pl.ds(d * quarter + j * part, part)]

    @pl.when(sec > 0)
    def _():
        send(grad, passed_ref.at[0], passed_send, passed_recv, sec - 1, dp)

    small[1].wait()
    small[2].wait()
    piece_of = lax.broadcasted_iota(jnp.int32, (pieces, tokens), 0)
    named = one_hot(piece_of, tok_ref[...])
    line_of = lax.broadcasted_iota(jnp.int32, (16, pieces), 0)
    home = home_ref[...]
    keeper_and_place = jnp.where(line_of == 0, home // ROWS, home % ROWS)
    found = dot(keeper_and_place.astype(F32).astype(BF16), named)
    keeper_row, place_row = found[0:1], found[1:2]
    sub = lax.broadcasted_iota(jnp.int32, (tokens, tokens), 0)
    lane = lax.broadcasted_iota(jnp.int32, (tokens, tokens), 1)

    def as_column(row):
        return jnp.sum(jnp.where(sub == lane, row, 0.0), axis=1, keepdims=True)

    keeper_col, place_col = as_column(keeper_row), as_column(place_row)
    same = keeper_col == keeper_row
    slot_row = jnp.max(jnp.where(same & (place_col < place_row), 1.0, 0.0), axis=0, keepdims=True)
    slot_col = jnp.max(jnp.where(same & (place_row < place_col), 1.0, 0.0), axis=1, keepdims=True)

    def split(keeper, way):
        keeper = keeper.astype(jnp.int32)
        kz, ky, kc = keeper // peers, (keeper // 2) % ring, keeper % 2
        return (ky, kz, kc) if way == 0 else (kz, ky, kc)

    def slot_index(keeper, slot, way):
        near, far, kc = split(keeper, way)
        return (near * 2 + kc) * peers + far * 2 + slot.astype(jnp.int32)

    slot_sub = lax.broadcasted_iota(jnp.int32, (all_slots, tokens), 0)
    slot_lane = lax.broadcasted_iota(jnp.int32, (tokens, all_slots), 1)
    place_lane = lax.broadcasted_iota(jnp.int32, (tokens, LANES), 1)
    for way in range(2):
        spread = one_hot(slot_sub, slot_index(keeper_row, slot_row, way))
        by_slot[way] = spread
        far_place = split(keeper_col, way)[1] * ROWS + place_col.astype(jnp.int32)
        meta_out[way] = jnp.minimum(dot(spread, one_hot(place_lane, far_place)), 1.0).astype(BF16)
        to_ring(way, way, meta_out, meta_in, meta_send, meta_recv)

    @pl.when(sec == sections - 1)
    def _():
        zeros[...] = jnp.zeros_like(zeros)
        for c in range(CHUNKS):
            rows = pl.ds(c * chunk, chunk)
            pltpu.make_async_copy(zeros, passed_ref.at[0, rows], zero_sem.at[c]).start()

    def slots(b):
        way = part_of(b) % 2

        def run():
            if b < PARTS:

                @pl.when(sec > 0)
                def _():
                    drain(grad_part.at[b], quarter_recv.at[b])

            slots_out[b] = dot(by_slot[way], grad_part[b]).astype(BF16)
            to_ring(way, b, slots_out, slots_in, slots_send, slots_recv)

        where_summed(b, run)

    def learn_places(way):
        ring_wait(way, meta_in, meta_recv)
        turned = meta_in[way].astype(F32).T[0:places].astype(BF16)
        meta_turned[way] = turned
        if way == 0:
            hits = dot(turned, jnp.ones((all_slots, LANES), BF16))
            none = jnp.zeros((ROWS, LANES), F32)
            packed = [x for q in range(ring) for x in (hits[q * ROWS : (q + 1) * ROWS], none)]
            part_out[0, :, pl.ds(mid, LANES)] = jnp.concatenate(packed, axis=0).astype(BF16)

    def part_cols(b):
        return pl.ds(0, mid + LANES if b == 0 else mid)

    def pack(rows):
        return jnp.concatenate([rows[:, 0:mid], rows[:, mid:part]], axis=0)

    def unpack(rows):
        return jnp.concatenate([rows[0:ROWS, 0:mid], rows[ROWS : 2 * ROWS, 0:mid]], axis=1)

    def parts(b):
        way = part_of(b) % 2
        cols = part_cols(b)

        def run():
            ring_wait(b, slots_in, slots_recv)
            sums = dot(meta_turned[way], slots_in[b])
            packed = [pack(sums[q * ROWS : (q + 1) * ROWS]) for q in range(ring)]
            part_out[b, :, pl.ds(0, mid)] = jnp.concatenate(packed, axis=0).astype(BF16)

            @pl.loop(0, ring - 1, unroll=True)
            def _(k):
                q = (line_me[way] + farthest_first(k, ring)) % ring
                theirs = pl.ds(pl.multiple_of(q * 2 * ROWS, 2 * ROWS), 2 * ROWS)
                send(
                    part_out.at[b, theirs, cols],
                    part_in.at[b, line_me[way], :, cols],
                    part_send.at[b],
                    part_recv.at[b],
                    sec,
                    line_peer[way](q),
                )

            mine = pl.ds(pl.multiple_of(line_me[way] * 2 * ROWS, 2 * ROWS), 2 * ROWS)
            part_in[b, line_me[way], :, cols] = part_out[b, mine, cols]

        where_summed(b, run)

    def total(b):
        drain(part_in.at[b, pl.ds(0, ring - 1), :, part_cols(b)], part_recv.at[b])
        rows = part_in[b, 0, :, part_cols(b)].astype(F32)
        for q in range(1, ring):
            rows += part_in[b, q, :, part_cols(b)].astype(F32)
        return rows

    def hand_total(e):
        @pl.when(sec == 0)
        def _():
            total_out[e] = unpack(total(PARTS + e))
            send(total_out.at[e], total_in.at[e], total_send.at[e], total_recv.at[e], EXTRA[e][0], dp)

    def update(j, hits):
        way = j % 2
        if has_no(j) is None:
            rows = total(j)
            sums = unpack(rows)
            if j == 0:
                hits = rows[0:ROWS, mid : mid + 1]
        else:

            def run():
                row_sums[...] = unpack(total(j))

            where_summed(j, run)
            for e, (d, k) in enumerate(EXTRA):
                if k == j:

                    @pl.when(sec == d)
                    def _():
                        drain(total_in.at[e], total_recv.at[e])
                        row_sums[...] = total_in[e]

            sums = row_sums[...]
        cols = pl.ds(j * part, part)
        table, first, second = adam_rows(
            hits > 0.5, sums, table_ref[:, cols], first_ref[:, cols], second_ref[:, cols]
        )
        rows_out[j] = pack(table).astype(BF16)

        @pl.loop(0, ring - 1, unroll=True)
        def _(k):
            q = (line_me[way] + farthest_first(k, ring)) % ring
            send(
                rows_out.at[j],
                rows_in.at[j, line_me[way]],
                rows_send.at[j],
                rows_recv.at[j],
                sec,
                line_peer[way](q),
            )

        rows_in[j, line_me[way]] = rows_out[j]
        new_table_ref[:, cols] = table
        new_first_ref[:, cols] = first
        new_second_ref[:, cols] = second
        return hits

    def give_back(j):
        way = j % 2
        drain(rows_in.at[j, pl.ds(0, ring - 1)], rows_recv.at[j])
        blocks = [unpack(rows_in[j, q].astype(F32)) for q in range(ring)]
        table = jnp.concatenate(blocks, axis=0).astype(BF16)
        back_out[j] = dot(meta_in[way, :, pl.ds(0, places)], table).astype(BF16)
        to_ring(way, j, back_out, back_in, back_send, back_recv)

    def fresh(j):
        ring_wait(j, back_in, back_recv)
        fresh_ref[:, pl.ds(j * part, part)] = dot(by_token[j % 2], back_in[j])

    def learn():
        for way in range(2):
            learn_places(way)
            by_token[way] = one_hot(slot_lane, slot_index(keeper_col, slot_col, way))
        for copy in small[3:]:
            copy.wait()

    buffers = (*range(PARTS, PARTS + len(EXTRA)), *range(PARTS))
    for b in buffers:
        slots(b)
    learn()
    for b in buffers:
        parts(b)
    hits = None
    for e in range(len(EXTRA)):
        hand_total(e)
    for j in range(PARTS):
        hits = update(j, hits)
    for j in range(PARTS):
        give_back(j)
    @pl.when(sec == 0)
    def _():
        drain(grad.at[:, pl.ds(0, width - quarter - len(EXTRA) * part)], quarter_send)

    @pl.when(sec > 0)
    def _():
        drain(grad, passed_send)

    @pl.when(sec < sections - 1)
    def _():
        drain(passed_ref.at[0], passed_recv)

    @pl.when(sec == sections - 1)
    def _():
        for c in range(CHUNKS):
            rows = pl.ds(c * chunk, chunk)
            pltpu.make_async_copy(zeros, passed_ref.at[0, rows], zero_sem.at[c]).wait()

    for way in range(2):
        ring_wait(way, meta_out, meta_send)
    for j in range(PARTS):
        drain(rows_in.at[j, pl.ds(0, ring - 1)], rows_send.at[j])
    for b in buffers:

        def sent():
            ring_wait(b, slots_out, slots_send)
            drain(part_in.at[b, pl.ds(0, ring - 1), :, part_cols(b)], part_send.at[b])

        where_summed(b, sent)

    @pl.when(sec == 0)
    def _():
        for e in range(len(EXTRA)):
            drain(total_out.at[e], total_send.at[e])

    for j in range(PARTS):
        fresh(j)
    for j in range(PARTS):
        ring_wait(j, back_out, back_send)


def hand_out(*refs):
    ins, outs, sems = refs[:5], refs[5:10], refs[10]
    copies = [pltpu.make_async_copy(a, b, sems.at[k]) for k, (a, b) in enumerate(zip(ins, outs))]
    for copy in copies:
        copy.start()
    for copy in copies:
        copy.wait()


def shards(
    ring,
    saved_input,
    upstream,
    cotangent,
    norm_gain,
    token_ids,
    piece_home,
    piece_table,
    first_moment,
    second_moment,
):
    _, tokens, width = saved_input.shape
    rows, quarter = piece_table.shape
    part = quarter // PARTS
    peers = 2 * ring
    slots = peers * peers
    hbm = pl.BlockSpec(memory_space=pltpu.HBM)
    anywhere = pl.BlockSpec(memory_space=pl.ANY)
    vmem = pl.BlockSpec(memory_space=pltpu.VMEM)
    dma = pltpu.SemaphoreType.DMA
    small = jax.ShapeDtypeStruct((rows, quarter), F32)
    out_shape = (
        jax.ShapeDtypeStruct((1, tokens, width), BF16),
        jax.ShapeDtypeStruct((tokens, quarter), F32),
        small,
        small,
        small,
    )
    arrays = (
        saved_input,
        upstream,
        cotangent,
        norm_gain,
        token_ids[None, :],
        piece_home[None, :],
        piece_table,
        first_moment,
        second_moment,
    )
    results = pl.pallas_call(
        functools.partial(kernel, ring),
        out_shape=out_shape,
        in_specs=[hbm] * 9,
        out_specs=(anywhere, vmem, vmem, vmem, vmem),
        scratch_shapes=[
            pltpu.VMEM((tokens, width), BF16),
            pltpu.VMEM((tokens, width), BF16),
            pltpu.VMEM((tokens, width), BF16),
            pltpu.VMEM((1, width), BF16),
            pltpu.VMEM((1, tokens), jnp.int32),
            pltpu.VMEM((1, piece_home.shape[0]), jnp.int32),
            pltpu.VMEM((rows, quarter), F32),
            pltpu.VMEM((rows, quarter), F32),
            pltpu.VMEM((rows, quarter), F32),
            pltpu.VMEM((tokens, width), BF16),
            pltpu.VMEM((tokens // CHUNKS, width), BF16),
            pltpu.VMEM((BUFFERS, tokens, part), BF16),
            pltpu.VMEM((2, slots, tokens), BF16),
            pltpu.VMEM((2, tokens, slots), BF16),
            pltpu.VMEM((2, slots, LANES), BF16),
            pltpu.VMEM((2, slots, LANES), BF16),
            pltpu.VMEM((2, ring * ROWS, slots), BF16),
            pltpu.VMEM((BUFFERS, slots, part), BF16),
            pltpu.VMEM((BUFFERS, slots, part), BF16),
            pltpu.VMEM((BUFFERS, ring * 2 * ROWS, part // 2 + LANES), BF16),
            pltpu.VMEM((BUFFERS, ring, 2 * ROWS, part // 2 + LANES), BF16),
            pltpu.VMEM((ROWS, part), F32),
            pltpu.VMEM((len(EXTRA), ROWS, part), F32),
            pltpu.VMEM((len(EXTRA), ROWS, part), F32),
            pltpu.VMEM((PARTS, 2 * ROWS, part // 2), BF16),
            pltpu.VMEM((PARTS, ring, 2 * ROWS, part // 2), BF16),
            pltpu.VMEM((PARTS, slots, part), BF16),
            pltpu.VMEM((PARTS, slots, part), BF16),
            dma((CHUNKS, 3)),
            dma((6,)),
            dma((CHUNKS,)),
            dma,
            dma((PARTS,)),
            dma,
            dma,
            dma((2,)),
            dma((2,)),
        ]
        + [dma((BUFFERS,))] * 4
        + [dma((PARTS,))] * 4
        + [dma((len(EXTRA),))] * 2,
        compiler_params=pltpu.CompilerParams(
            collective_id=0, has_side_effects=True, vmem_limit_bytes=40 * 2**20
        ),
        cost_estimate=pl.CostEstimate(
            flops=2 * 10**8, bytes_accessed=6 * 2**20, transcendentals=0
        ),
    )(*(pltpu.with_memory_space_constraint(array, pltpu.HBM) for array in arrays))
    return pl.pallas_call(
        hand_out,
        out_shape=out_shape,
        in_specs=[anywhere] * 5,
        out_specs=(hbm,) * 5,
        scratch_shapes=[dma((5,))],
        compiler_params=pltpu.CompilerParams(vmem_limit_bytes=40 * 2**20),
        cost_estimate=pl.CostEstimate(flops=0, bytes_accessed=3 * 2**20, transcendentals=0),
    )(*results)


def solution(mesh):
    ring = math.isqrt(mesh.shape["dp"] // 2)
    in_specs = (
        P("section", "dp", None),
        P("section", "dp", None),
        P("section", "dp", None),
        P("section", None),
        P("dp"),
        P(),
        P("dp", "section"),
        P("dp", "section"),
        P("dp", "section"),
    )
    out_specs = (
        P("section", "dp", None),
        P("dp", "section"),
        P("dp", "section"),
        P("dp", "section"),
        P("dp", "section"),
    )
    return jax.shard_map(
        functools.partial(shards, ring),
        mesh=mesh,
        in_specs=in_specs,
        out_specs=out_specs,
        check_vma=False,
    )
```
